256 devices in a mesh: segment: 8 (over z), dp: 32 (over x, y, core).
Axes of the slice: x: 4, y: 4, z: 8, core: 2. Of those that a mesh axis runs over, the one named last changes fastest.
Arguments:
- images: bfloat16 [4, 64, 64, 256], P(None, 'dp'), may hold values from -6 to 6
- cotangent: bfloat16 [4, 64, 64, 256], P(None, 'dp'), may hold values from -0.059814453 to 0.059814453
- section_cells: int32 [8], replicated, may hold values from 1 to 8, as said below
- point_weight: bfloat16 [64, 256, 256], P('segment'), may hold values from -0.0625 to 0.0625
- tap_weight: float32 [64, 3, 256], P('segment'), may hold values from -3 to 3
Outputs:
- grad_point: float32 [64, 256, 256], P('segment', 'dp')
- grad_taps: float32 [64, 3, 256], P('segment')
The draws below stay inside these ranges and needn't reach their ends.
Inputs may be any that keep to these rules, and one draw needn't show every extreme that they name: `section_cells`: every section has at least one live slot, and in every draw some section has all 8 slots live.
All inputs are finite; a program needn't handle non-finite values.
Results may differ from the reference program's by a relative error of at most 0.015.
The reference program's roundings to bfloat16 on the way count: a program that leaves them out, or rounds other values in their place, can miss the bound.
Values may be sent and summed in bfloat16 or wider, within the bound.
A program may use at most 64 MiB of HBM per device.

```python
import jax
import jax.numpy as jnp
from jax import lax

C = 256
W = 64
MICRO = 4
CELLS_DEV = 8
CELLS = 64
ROWS = 64
N_SEGMENT = 8


def draw_section_cells(key, part):
    first_key = jax.random.fold_in(key, 11)
    second_key = jax.random.fold_in(key, 12)
    drawn = jax.random.randint(first_key, (N_SEGMENT,), 1, CELLS_DEV + 1)
    fullest = jax.random.randint(second_key, (), 0, N_SEGMENT)
    return jnp.where(jnp.arange(N_SEGMENT) == fullest, CELLS_DEV, drawn).astype(jnp.int32)


def with_spikes(array, rng, source, target, shards_of, factor):
    owner, partner = [(jnp.arange(array.shape[axis_at]) // (array.shape[axis_at] // shards_of)).reshape([-1 if axis == axis_at else 1 for axis in range(array.ndim)]) for axis_at in (source, target)]
    chosen = jax.random.permutation(rng, shards_of)[partner]
    strong = (owner == chosen) | (owner == (partner + shards_of // 2) % shards_of)
    return jnp.where(strong, factor * array, array)


def shard_levels(stream_key, shape, shards, least, high):
    factor_of = 1.0
    for dim, blocks in shards:
        steps = jax.random.uniform(jax.random.fold_in(jax.random.fold_in(stream_key, 6), dim), (blocks,), jnp.float32, least / len(shards), high / len(shards))
        factor_of = factor_of * jnp.repeat(jnp.exp(steps), shape[dim] // blocks).reshape((-1,) + (1,) * (len(shape) - 1 - dim))
    return factor_of


def scatter_about(stream_key, dims, scale, bound, cuts=(), dtype=jnp.bfloat16):
    loudness = shard_levels(stream_key, dims, cuts, -0.22, 0.18) if cuts else 1.0
    entries = jax.random.normal(stream_key, dims, jnp.float32) * scale * loudness
    return jnp.minimum(jnp.maximum(entries, -bound), bound).astype(dtype)


def gaussian_with(key, extent, deviation, limit, split, heavy, held_as=jnp.bfloat16):
    values = deviation * jax.random.normal(key, extent, jnp.float32)
    if split:
        values = values * shard_levels(key, extent, split, -0.22, 0.18)
    return jnp.clip(with_spikes(values, jax.random.fold_in(key, 3), *heavy), -limit, limit).astype(held_as)


def setup_inputs(seed: int = 0) -> dict:
    arg_keys = jax.random.split(jax.random.key(seed), 6)
    return {
        "images": gaussian_with(arg_keys[0], (MICRO, ROWS, W, C), 1.0, 6.0, ((1, 32),), (1, 3, 32, 2.75)),
        "cotangent": scatter_about(arg_keys[1], (MICRO, ROWS, W, C), 0.01, 0.059814453, ((1, 32),)),
        "section_cells": draw_section_cells(jax.random.fold_in(arg_keys[5], 71), 0),
        "point_weight": scatter_about(arg_keys[3], (CELLS, C, C), (CELLS * C // 2) ** -0.5, 0.0625, ((0, 8),)),
        "tap_weight": scatter_about(arg_keys[4], (CELLS, 3, C), 0.5, 3.0, ((0, 8),), jnp.float32),
    }


def shifted(values, dilation):
    padding = jnp.zeros_like(values[:, :dilation, :])
    before = jnp.concatenate([padding, values[:, :-dilation, :]], axis=1)
    beyond = jnp.concatenate([values[:, dilation:, :], padding], axis=1)
    return before, beyond


def cell_inner(incoming, tap_rows, dilation):
    values = incoming.astype(jnp.float32)
    before, beyond = shifted(values, dilation)
    hidden = tap_rows[0] * before + tap_rows[1] * values + tap_rows[2] * beyond
    activated = (hidden * jax.nn.sigmoid(hidden)).astype(jnp.bfloat16)
    return values, before, beyond, hidden, activated


def cell_forward(incoming, tap_rows, matrix, dilation):
    values, before, beyond, hidden, activated = cell_inner(incoming, tap_rows, dilation)
    channels = matrix.shape[0]
    branch = jnp.dot(activated.reshape(-1, channels), matrix, preferred_element_type=jnp.float32)
    return (values + branch.reshape(values.shape)).astype(jnp.bfloat16)


def cell_backward(incoming, tap_rows, matrix, dilation, upstream):
    values, before, beyond, hidden, activated = cell_inner(incoming, tap_rows, dilation)
    channels = matrix.shape[0]
    flat_grad = upstream.astype(jnp.bfloat16).reshape(-1, channels)
    grad_matrix = lax.dot_general(activated.reshape(-1, channels), flat_grad, (((0,), (0,)), ((), ())), preferred_element_type=jnp.float32)
    grad_active = lax.dot_general(flat_grad, matrix, (((1,), (1,)), ((), ())), preferred_element_type=jnp.float32).reshape(values.shape)
    sigmoid_part = jax.nn.sigmoid(hidden)
    grad_hidden = grad_active * sigmoid_part * (1.0 + hidden * (1.0 - sigmoid_part))
    grad_tap = jnp.stack([jnp.sum(grad_hidden * before, axis=(0, 1)), jnp.sum(grad_hidden * values, axis=(0, 1)), jnp.sum(grad_hidden * beyond, axis=(0, 1))])
    spread_before, spread_beyond = shifted(grad_hidden, dilation)
    grad_in = upstream + tap_rows[0] * spread_beyond + tap_rows[1] * grad_hidden + tap_rows[2] * spread_before
    return grad_in, grad_matrix, grad_tap


def reference(images, cotangent, section_cells, point_weight, tap_weight):
    cell_count = point_weight.shape[0]
    channels = point_weight.shape[1]
    positions = jnp.arange(cell_count).astype(jnp.int32)
    section_of = positions // CELLS_DEV
    live_cells = (positions % CELLS_DEV) < section_cells[section_of]
    pair_live = live_cells.reshape(cell_count // 2, 2)
    pair_matrix = point_weight.reshape(cell_count // 2, 2, channels, channels)
    pair_taps = tap_weight.reshape(cell_count // 2, 2, 3, channels)
    total_point = jnp.zeros((cell_count, channels, channels), jnp.float32)
    total_taps = jnp.zeros((cell_count, 3, channels), jnp.float32)

    def forward_pair(running, pieces):
        matrices, taps_pair, active_flags = pieces
        stored = []
        for within in range(2):
            stored.append(running)
            produced = cell_forward(running, taps_pair[within], matrices[within], 1 + within)
            running = jnp.where(active_flags[within], produced, running)
        return running, jnp.stack(stored)

    def backward_pair(upstream, pieces):
        matrices, taps_pair, active_flags, inputs_pair = pieces
        point_parts = [None, None]
        tap_parts = [None, None]
        for within in (1, 0):
            grad_in, grad_matrix, grad_tap = cell_backward(inputs_pair[within], taps_pair[within], matrices[within], 1 + within, upstream)
            upstream = jnp.where(active_flags[within], grad_in, upstream)
            point_parts[within] = jnp.where(active_flags[within], grad_matrix, 0.0)
            tap_parts[within] = jnp.where(active_flags[within], grad_tap, 0.0)
        return upstream, (jnp.stack(point_parts), jnp.stack(tap_parts))

    for micro_index in range(MICRO):
        last_output, kept_inputs = lax.scan(forward_pair, images[micro_index], (pair_matrix, pair_taps, pair_live))
        first_grad, grads_pair = lax.scan(backward_pair, cotangent[micro_index].astype(jnp.float32), (pair_matrix, pair_taps, pair_live, kept_inputs), reverse=True)
        total_point = total_point + grads_pair[0].reshape(cell_count, channels, channels)
        total_taps = total_taps + grads_pair[1].reshape(cell_count, 3, channels)
    return total_point, total_taps
```

```python
import jax
import jax.numpy as jnp
from jax import lax
from jax.experimental import pallas as pl
from jax.experimental.pallas import tpu as pltpu
from jax.sharding import PartitionSpec as P

SECTION = 8
PLANES = 8
SIDE = 4
WIDTH = 64
CHANNELS = 256
HALF = CHANNELS // 2
QUARTER = CHANNELS // 4
LAG_SUM = 1
LAG_FIRST = 3
LAG_SECOND = 5


def neighbours(values, dilation):
    count = values.shape[0]
    place = lax.broadcasted_iota(jnp.int32, values.shape, 0)
    before = jnp.where(place >= dilation, pltpu.roll(values, dilation, 0), 0.0)
    beyond = jnp.where(place < count - dilation, pltpu.roll(values, count - dilation, 0), 0.0)
    return before, beyond


def window_kernel(
    section_cells, images, cotangent, point_weight, tap_weight,
    out_point, out_taps,
    weight, taps, inputs, active, slope, image, grad_row, x_now, g_now,
    partial, from_twin, paired, first_a, first_b, joined_a, joined_b,
    second_a, second_b, square, planes,
    tap_grads, tap_planes, tap_twin, tap_x, tap_y, tap_final,
    local_sem,
    gz_send, gz_recv, g1_send, g1_recv, g2_send, g2_recv, gt_send, gt_recv,
    rt_send, rt_recv, r1_send, r1_recv, r2_send, r2_recv, r3_send, r3_recv,
    tz_send, tz_recv, te_send, te_recv,
):
    z = lax.axis_index("segment")
    dp = lax.axis_index("dp")
    x, y, core = dp // 8, (dp // 2) % SIDE, dp % 2

    def device(dz=0, dx=0, dy=0, dc=0):
        px, py = (x + dx + SIDE) % SIDE, (y + dy + SIDE) % SIDE
        return ((z + dz + PLANES) % PLANES, (px * SIDE + py) * 2 + (core + dc) % 2)

    twin = device(dc=1)

    def remote(src, dst, send, recv, target):
        return pltpu.make_async_remote_copy(
            src_ref=src, dst_ref=dst, send_sem=send, recv_sem=recv,
            device_id=target, device_id_type=pl.DeviceIdType.MESH,
        )

    own_row = pltpu.make_async_copy(images.at[z // 2, z % 2], image, local_sem.at[0])
    own_grad = pltpu.make_async_copy(cotangent.at[z // 2, z % 2], grad_row, local_sem.at[1])
    own_weight = pltpu.make_async_copy(
        point_weight, weight.at[pl.ds(z * SECTION, SECTION)], local_sem.at[2]
    )
    own_row.start()
    own_grad.start()
    own_weight.start()
    for member in range(SECTION):
        for tap in range(3):
            taps[z, tap, member : member + 1, :] = tap_weight[member, tap : tap + 1, :]

    barrier = pltpu.get_barrier_semaphore()
    partners = [twin]
    partners += [device(dz=step) for step in range(1, PLANES)]
    partners += [device(dx=step) for step in range(1, SIDE)]
    partners += [device(dy=step) for step in range(1, SIDE)]
    for partner in partners:
        pl.semaphore_signal(
            barrier, inc=1, device_id=partner, device_id_type=pl.DeviceIdType.MESH
        )
    pl.semaphore_wait(barrier, len(partners))

    base = core * HALF
    rows_a = pl.ds(pl.multiple_of(base + (y % 2) * QUARTER, QUARTER), QUARTER)
    rows_b = pl.ds(pl.multiple_of(base + (x % 2) * QUARTER, QUARTER), QUARTER)
    other_a = pl.ds(pl.multiple_of(base + (1 - y % 2) * QUARTER, QUARTER), QUARTER)
    other_b = pl.ds(pl.multiple_of(base + (1 - x % 2) * QUARTER, QUARTER), QUARTER)
    rows_core = pl.ds(pl.multiple_of(base, HALF), HALF)
    rows_twin = pl.ds(pl.multiple_of(HALF - base, HALF), HALF)
    lanes_core, lanes_twin = rows_core, rows_twin

    def over_planes(step):
        target = device(dz=step)
        return (
            remote(
                point_weight.at[x, rows_a], weight.at[z * SECTION + x, rows_a],
                gz_send.at[step, 0], gz_recv.at[z, 0], target,
            ),
            remote(
                point_weight.at[SIDE + y, rows_b], weight.at[z * SECTION + SIDE + y, rows_b],
                gz_send.at[step, 1], gz_recv.at[z, 1], target,
            ),
            remote(
                taps.at[z, :, :, lanes_core], taps.at[z, :, :, lanes_core],
                gz_send.at[step, 2], gz_recv.at[z, 2], target,
            ),
        )

    def arrived(ref, sem):
        pltpu.make_async_copy(ref, ref, sem).wait()

    def along_side(s, step):
        piece_a = weight.at[s * SECTION + x, rows_a]
        piece_b = weight.at[s * SECTION + SIDE + y, rows_b]
        return (
            remote(piece_a, piece_a, g1_send.at[s, step, 0], g1_recv.at[s, step, 0], device(dx=step)),
            remote(piece_b, piece_b, g1_send.at[s, step, 1], g1_recv.at[s, step, 1], device(dy=step)),
        )

    def across_side(s):
        copies = []
        for low, direction in ((0, 1), (2, -1)):
            piece_a = weight.at[pl.ds(s * SECTION + low, 2), rows_a]
            piece_b = weight.at[pl.ds(s * SECTION + SIDE + low, 2), rows_b]
            at = low // 2
            copies.append(
                remote(piece_a, piece_a, g2_send.at[s, at, 0], g2_recv.at[s, at, 0], device(dy=direction))
            )
            copies.append(
                remote(piece_b, piece_b, g2_send.at[s, at, 1], g2_recv.at[s, at, 1], device(dx=direction))
            )
        return copies

    def to_twin(s):
        half = weight.at[pl.ds(s * SECTION, SECTION), rows_core]
        lanes = taps.at[s, :, :, lanes_core]
        return (
            remote(half, half, gt_send.at[s, 0], gt_recv.at[s, 0], twin),
            remote(lanes, lanes, gt_send.at[s, 1], gt_recv.at[s, 1], twin),
        )

    for step in (4, 3, 5, 2, 6, 1, 7):
        for copy in over_planes(step):
            copy.start()

    def forward(s, slot, member, dilation, field):
        live = jnp.where(member < section_cells[s], 1.0, 0.0)
        values = field.astype(jnp.float32)
        before, beyond = neighbours(values, dilation)
        rows = [taps[s, tap, pl.ds(member, 1), :] for tap in range(3)]
        hidden = rows[0] * before + rows[1] * values + rows[2] * beyond
        sigmoid = 0.5 * jnp.tanh(0.5 * hidden) + 0.5
        product = hidden * sigmoid
        activated = (product * live).astype(jnp.bfloat16)
        inputs[slot] = field
        active[slot] = activated
        slope[slot] = (sigmoid + product * (1.0 - sigmoid)) * live
        branch = jnp.dot(activated, weight[slot], preferred_element_type=jnp.float32)
        return (values + branch).astype(jnp.bfloat16)

    own_row.wait()
    x_now[...] = image[...]

    def gather_step(t, carry):
        @pl.when((t < PLANES) & (t != z))
        def _():
            arrived(weight.at[t * SECTION + x, rows_a], gz_recv.at[t, 0])
            arrived(weight.at[t * SECTION + SIDE + y, rows_b], gz_recv.at[t, 1])
            for step in range(1, SIDE):
                for copy in along_side(t, step):
                    copy.start()

        s1 = t - 1

        @pl.when((s1 >= 0) & (s1 < PLANES) & (s1 != z))
        def _():
            for step in range(1, SIDE):
                arrived(
                    weight.at[s1 * SECTION + (x + SIDE - step) % SIDE, rows_a], g1_recv.at[s1, step, 0]
                )
                arrived(
                    weight.at[s1 * SECTION + SIDE + (y + SIDE - step) % SIDE, rows_b],
                    g1_recv.at[s1, step, 1],
                )
            for copy in across_side(s1):
                copy.start()

        s2 = t - 2

        @pl.when((s2 >= 0) & (s2 < PLANES) & (s2 != z))
        def _():
            for low in (0, 2):
                arrived(weight.at[pl.ds(s2 * SECTION + low, 2), other_a], g2_recv.at[s2, low // 2, 0])
                arrived(
                    weight.at[pl.ds(s2 * SECTION + SIDE + low, 2), other_b],
                    g2_recv.at[s2, low // 2, 1],
                )
            arrived(taps.at[s2, :, :, lanes_core], gz_recv.at[s2, 2])
            for copy in to_twin(s2):
                copy.start()

        s3 = t - 3

        @pl.when(s3 >= 0)
        def _():
            @pl.when(s3 != z)
            def _():
                arrived(weight.at[pl.ds(s3 * SECTION, SECTION), rows_twin], gt_recv.at[s3, 0])
                arrived(taps.at[s3, :, :, lanes_twin], gt_recv.at[s3, 1])

            @pl.when(s3 == z)
            def _():
                own_weight.wait()

            def pair(p, field):
                slot = s3 * SECTION + 2 * p
                field = forward(s3, slot, 2 * p, 1, field)
                return forward(s3, slot + 1, 2 * p + 1, 2, field)

            x_now[...] = lax.fori_loop(0, SECTION // 2, pair, x_now[...])

        return carry

    lax.fori_loop(0, PLANES + 3, gather_step, 0)

    def pair_exchange(s):
        return remote(
            partial.at[s, :, :, 1 - core], from_twin.at[s], rt_send.at[s], rt_recv.at[s], twin
        )

    low, high = pl.ds(0, WIDTH // 2), pl.ds(WIDTH // 2, WIDTH // 2)

    def first_exchange(s, step):
        return (
            remote(
                paired.at[s, (x + step) % SIDE, :, low], first_a.at[s, step - 1],
                r1_send.at[s, step, 0], r1_recv.at[s, step, 0], device(dx=step),
            ),
            remote(
                paired.at[s, :, (y + step) % SIDE, high], first_b.at[s, step - 1],
                r1_send.at[s, step, 1], r1_recv.at[s, step, 1], device(dy=step),
            ),
        )

    def second_exchange(s, step):
        return (
            remote(
                joined_a.at[s, (y + step) % SIDE], second_a.at[s, step - 1],
                r2_send.at[s, step, 0], r2_recv.at[s, step, 0], device(dy=step),
            ),
            remote(
                joined_b.at[s, (x + step) % SIDE], second_b.at[s, step - 1],
                r2_send.at[s, step, 1], r2_recv.at[s, step, 1], device(dx=step),
            ),
        )

    def to_plane(s):
        return remote(
            square.at[s], planes.at[z], r3_send.at[s], r3_recv.at[z], (s, dp)
        )

    def taps_to_plane(s):
        return remote(
            tap_grads.at[s], tap_planes.at[z], tz_send.at[s], tz_recv.at[z], (s, dp)
        )

    def backward(s, slot, member, dilation, upstream):
        rounded = upstream.astype(jnp.bfloat16)
        grad_active = lax.dot_general(
            rounded, weight[slot], (((1,), (1,)), ((), ())), preferred_element_type=jnp.float32
        )
        grad_hidden = grad_active * slope[slot]
        spread_before, spread_beyond = neighbours(grad_hidden, dilation)
        values = inputs[slot].astype(jnp.float32)
        for tap, spread in enumerate((spread_beyond, grad_hidden, spread_before)):
            tap_grads[s, tap, pl.ds(member, 1), :] = jnp.sum(spread * values, axis=0, keepdims=True)
        grad_matrix = lax.dot_general(
            active[slot], rounded, (((0,), (0,)), ((), ())), preferred_element_type=jnp.float32
        )
        rows = [taps[s, tap, pl.ds(member, 1), :] for tap in range(3)]
        passed = (
            upstream + rows[0] * spread_beyond + rows[1] * grad_hidden + rows[2] * spread_before
        )
        return passed, grad_matrix.reshape(PLANES * SIDE, SECTION, CHANNELS)

    own_grad.wait()
    g_now[...] = grad_row[...].astype(jnp.float32)

    def wide(ref, *index):
        return ref[index].astype(jnp.float32)

    def backward_step(t, carry):
        @pl.when(t < PLANES)
        def _():
            s = PLANES - 1 - t

            def pair(step, upstream):
                p = SECTION // 2 - 1 - step
                slot = s * SECTION + 2 * p
                upstream, odd = backward(s, slot + 1, 2 * p + 1, 2, upstream)
                upstream, even = backward(s, slot, 2 * p, 1, upstream)
                both = jnp.concatenate([even, odd], axis=1).astype(jnp.bfloat16)
                partial[s, :, :, :, pl.ds(pl.multiple_of(16 * p, 16), 16), :] = both.reshape(
                    SIDE, SIDE, 2, 16, CHANNELS
                )
                return upstream

            g_now[...] = lax.fori_loop(0, SECTION // 2, pair, g_now[...])
            pair_exchange(s).start()

            @pl.when(s != z)
            def _():
                taps_to_plane(s).start()

            @pl.when(s == z)
            def _():
                tap_planes[z] = tap_grads[z]

        s1 = PLANES - 1 - (t - LAG_SUM)

        @pl.when((s1 >= 0) & (s1 < PLANES))
        def _():
            arrived(from_twin.at[s1], rt_recv.at[s1])

            def add(i, carry):
                paired[s1, i] = (wide(partial, s1, i, slice(None), core) + wide(from_twin, s1, i)).astype(
                    jnp.bfloat16
                )
                return carry

            lax.fori_loop(0, SIDE, add, 0)
            for step in range(1, SIDE):
                for copy in first_exchange(s1, step):
                    copy.start()

        s2 = PLANES - 1 - (t - LAG_FIRST)

        @pl.when((s2 >= 0) & (s2 < PLANES))
        def _():
            for step in range(1, SIDE):
                arrived(first_a.at[s2, step - 1], r1_recv.at[s2, step, 0])
                arrived(first_b.at[s2, step - 1], r1_recv.at[s2, step, 1])
            total_a = paired[s2, x, :, : WIDTH // 2, :].astype(jnp.float32)
            total_b = paired[s2, :, y, WIDTH // 2 :, :].astype(jnp.float32)
            for step in range(SIDE - 1):
                total_a += wide(first_a, s2, step)
                total_b += wide(first_b, s2, step)
            joined_a[s2] = total_a.astype(jnp.bfloat16)
            joined_b[s2] = total_b.astype(jnp.bfloat16)
            for step in range(1, SIDE):
                for copy in second_exchange(s2, step):
                    copy.start()

        s3 = PLANES - 1 - (t - LAG_SECOND)

        @pl.when((s3 >= 0) & (s3 < PLANES))
        def _():
            for step in range(1, SIDE):
                arrived(second_a.at[s3, step - 1], r2_recv.at[s3, step, 0])
                arrived(second_b.at[s3, step - 1], r2_recv.at[s3, step, 1])
            total_a = wide(joined_a, s3, y)
            total_b = wide(joined_b, s3, x)
            for step in range(SIDE - 1):
                total_a += wide(second_a, s3, step)
                total_b += wide(second_b, s3, step)
            total = jnp.concatenate([total_a, total_b], axis=0).astype(jnp.bfloat16)

            @pl.when(s3 != z)
            def _():
                square[s3] = total
                to_plane(s3).start()

            @pl.when(s3 == z)
            def _():
                planes[z] = total

        return carry

    lax.fori_loop(0, PLANES + LAG_SECOND, backward_step, 0)

    def others(body):
        def visit(s, carry):
            @pl.when(s != z)
            def _():
                body(s)

            return carry

        lax.fori_loop(0, PLANES, visit, 0)

    others(lambda s: arrived(tap_planes.at[s], tz_recv.at[s]))
    total = tap_planes[0]
    for s in range(1, PLANES):
        total += tap_planes[s]
    tap_twin[core] = total
    swap = remote(tap_twin.at[core], tap_twin.at[core], te_send.at[0, 0], te_recv.at[0, 0], twin)
    swap.start()
    arrived(tap_twin.at[1 - core], te_recv.at[0, 0])
    tap_x[x] = tap_twin[0, :, :, lanes_core] + tap_twin[1, :, :, lanes_core]

    def tap_side(buffer, place, step, at, **offset):
        return remote(
            buffer.at[place], buffer.at[place], te_send.at[at, step], te_recv.at[at, step],
            device(**offset),
        )

    for step in range(1, SIDE):
        tap_side(tap_x, x, step, 1, dx=step).start()
    for step in range(1, SIDE):
        arrived(tap_x.at[(x + SIDE - step) % SIDE], te_recv.at[1, step])
    tap_y[y] = (tap_x[0] + tap_x[1]) + (tap_x[2] + tap_x[3])
    for step in range(1, SIDE):
        tap_side(tap_y, y, step, 2, dy=step).start()
    for step in range(1, SIDE):
        arrived(tap_y.at[(y + SIDE - step) % SIDE], te_recv.at[2, step])
    tap_final[core] = (tap_y[0] + tap_y[1]) + (tap_y[2] + tap_y[3])
    last = remote(tap_final.at[core], tap_final.at[core], te_send.at[3, 0], te_recv.at[3, 0], twin)
    last.start()

    others(lambda s: arrived(planes.at[s], r3_recv.at[s]))
    total = wide(planes, 0)
    for s in range(1, PLANES):
        total += wide(planes, s)
    out_point[...] = total.reshape(SECTION, SECTION, CHANNELS)
    arrived(tap_final.at[1 - core], te_recv.at[3, 0])
    for member in range(SECTION):
        for tap in range(3):
            for side in range(2):
                out_taps[member, tap : tap + 1, side * HALF : (side + 1) * HALF] = tap_final[
                    side, tap, member : member + 1, :
                ]

    for step in range(1, PLANES):
        for copy in over_planes(step):
            copy.wait_send()

    def left(s):
        for step in range(1, SIDE):
            for copy in along_side(s, step):
                copy.wait_send()
        for copy in across_side(s):
            copy.wait_send()
        for copy in to_twin(s):
            copy.wait_send()
        taps_to_plane(s).wait_send()
        to_plane(s).wait_send()

    others(left)

    def left_sums(s, carry):
        pair_exchange(s).wait_send()
        for step in range(1, SIDE):
            for copy in first_exchange(s, step) + second_exchange(s, step):
                copy.wait_send()
        return carry

    lax.fori_loop(0, PLANES, left_sums, 0)
    swap.wait_send()
    for step in range(1, SIDE):
        tap_side(tap_x, x, step, 1, dx=step).wait_send()
        tap_side(tap_y, y, step, 2, dy=step).wait_send()
    last.wait_send()


def per_device(images, cotangent, section_cells, point_weight, tap_weight):
    cells = PLANES * SECTION
    bf16, f32 = jnp.bfloat16, jnp.float32
    vmem, dma = pltpu.VMEM, pltpu.SemaphoreType.DMA
    hbm_spec = pl.BlockSpec(memory_space=pl.ANY)
    vmem_spec = pl.BlockSpec(memory_space=pltpu.VMEM)
    block = (WIDTH, CHANNELS)
    half_block = (WIDTH // 2, CHANNELS)
    tap_block = (3, SECTION, CHANNELS)
    tap_half = (3, SECTION, HALF)
    scratch = [
        vmem((cells, CHANNELS, CHANNELS), bf16),
        vmem((PLANES,) + tap_block, f32),
        vmem((cells,) + block, bf16),
        vmem((cells,) + block, bf16),
        vmem((cells,) + block, f32),
        vmem(block, bf16),
        vmem(block, bf16),
        vmem(block, bf16),
        vmem(block, f32),
        vmem((PLANES, SIDE, SIDE, 2) + block, bf16),
        vmem((PLANES, SIDE, SIDE) + block, bf16),
        vmem((PLANES, SIDE, SIDE) + block, bf16),
        vmem((PLANES, SIDE - 1, SIDE) + half_block, bf16),
        vmem((PLANES, SIDE - 1, SIDE) + half_block, bf16),
        vmem((PLANES, SIDE) + half_block, bf16),
        vmem((PLANES, SIDE) + half_block, bf16),
        vmem((PLANES, SIDE - 1) + half_block, bf16),
        vmem((PLANES, SIDE - 1) + half_block, bf16),
        vmem((PLANES,) + block, bf16),
        vmem((PLANES,) + block, bf16),
        vmem((PLANES,) + tap_block, f32),
        vmem((PLANES,) + tap_block, f32),
        vmem((2,) + tap_block, f32),
        vmem((SIDE,) + tap_half, f32),
        vmem((SIDE,) + tap_half, f32),
        vmem((2,) + tap_half, f32),
        dma((3,)),
    ]
    for shape in (
        (PLANES, 3), (PLANES, SIDE, 2), (PLANES, 2, 2), (PLANES, 2),
        (PLANES,), (PLANES, SIDE, 2), (PLANES, SIDE, 2), (PLANES,),
        (PLANES,), (SIDE, SIDE),
    ):
        scratch += [dma(shape), dma(shape)]
    return pl.pallas_call(
        window_kernel,
        out_shape=(
            jax.ShapeDtypeStruct((SECTION, SECTION, CHANNELS), f32),
            jax.ShapeDtypeStruct((SECTION, 3, CHANNELS), f32),
        ),
        in_specs=[pl.BlockSpec(memory_space=pltpu.SMEM), hbm_spec, hbm_spec, hbm_spec, vmem_spec],
        out_specs=(vmem_spec, vmem_spec),
        scratch_shapes=scratch,
        compiler_params=pltpu.CompilerParams(
            collective_id=0, has_side_effects=True, vmem_limit_bytes=56 << 20
        ),
    )(section_cells, images, cotangent, point_weight, tap_weight)


def solution(mesh):
    placed = (
        P(None, "dp", None, None),
        P(None, "dp", None, None),
        P(),
        P("segment", None, None),
        P("segment", None, None),
    )
    return jax.shard_map(
        per_device,
        mesh=mesh,
        in_specs=placed,
        out_specs=(P("segment", "dp", None), P("segment", None, None)),
        check_vma=False,
    )
```

```python
import jax
import jax.numpy as jnp
from jax import lax
from jax.experimental import pallas as pl
from jax.experimental.pallas import tpu as pltpu
from jax.sharding import PartitionSpec as P

SECTION = 8
PLANES = 8
SIDE = 4
WIDTH = 64
CHANNELS = 256
HALF = CHANNELS // 2
QUARTER = CHANNELS // 4
EIGHTH = CHANNELS // 8
MOST_RUNS = 1
RING_STEPS = (0, 2, 3, 4)
LAG_SUM = 1
LAG_NEAR = 2
LAG_FIRST = 4
LAG_SECOND = 6
LAG_ACROSS = 2
LAG_TWIN = 4
VISITS = PLANES - 1 + LAG_TWIN


def arrival_orders():
    orders, runs = [], []
    for plane in range(PLANES):
        left = [s for s in range(PLANES) if s != plane]
        hops = {s: min((s - plane) % PLANES, (plane - s) % PLANES) for s in left}
        order = []
        while left:
            reach = sum(step <= len(order) for step in RING_STEPS)
            order.append(min(s for s in left if hops[s] <= reach))
            left.remove(order[-1])
        done, counts = 0, []
        for step in range(VISITS):
            count = 0
            while done < PLANES and (done == plane or order.index(done) < step - LAG_TWIN):
                if count == MOST_RUNS:
                    break
                count, done = count + 1, done + 1
            counts.append(count)
        orders.append(sum(s * 8**i for i, s in enumerate(order)))
        runs.append(sum(n * 4**i for i, n in enumerate(counts)))
    return orders, runs


def by_plane(z, values):
    chosen = values[0]
    for plane in range(1, PLANES):
        chosen = jnp.where(z == plane, values[plane], chosen)
    return chosen


def neighbours(values, dilation):
    count = values.shape[0]
    place = lax.broadcasted_iota(jnp.int32, values.shape, 0)
    before = jnp.where(place >= dilation, pltpu.roll(values, dilation, 0), 0.0)
    beyond = jnp.where(place < count - dilation, pltpu.roll(values, count - dilation, 0), 0.0)
    return before, beyond


def window_kernel(
    section_cells, images, cotangent, point_weight, tap_weight,
    out_point, out_taps,
    weight, taps, inputs, active, slope, image, grad_row, x_now, g_now,
    partial, from_twin, paired, far_a, far_b, first_a, first_b, joined_a, joined_b,
    second_a, second_b, square, planes,
    tap_grads, tap_planes, tap_twin, tap_x, tap_y, tap_final,
    local_sem,
    gz_send, gz_recv, g1_send, g1_recv, g2_send, g2_recv, gt_send, gt_recv,
    rt_send, rt_recv, rf_send, rf_recv, r1_send, r1_recv, r2_send, r2_recv, r3_send, r3_recv,
    tz_send, tz_recv, te_send, te_recv,
):
    z = lax.axis_index("segment")
    dp = lax.axis_index("dp")
    x, y, core = dp // 8, (dp // 2) % SIDE, dp % 2

    def device(dz=0, dx=0, dy=0, dc=0):
        px, py = (x + dx + SIDE) % SIDE, (y + dy + SIDE) % SIDE
        return ((z + dz + PLANES) % PLANES, (px * SIDE + py) * 2 + (core + dc) % 2)

    twin = device(dc=1)

    def remote(src, dst, send, recv, target):
        return pltpu.make_async_remote_copy(
            src_ref=src, dst_ref=dst, send_sem=send, recv_sem=recv,
            device_id=target, device_id_type=pl.DeviceIdType.MESH,
        )

    own_row = pltpu.make_async_copy(images.at[z // 2, z % 2], image, local_sem.at[0])
    own_grad = pltpu.make_async_copy(cotangent.at[z // 2, z % 2], grad_row, local_sem.at[1])
    own_weight = pltpu.make_async_copy(
        point_weight, weight.at[pl.ds(z * SECTION, SECTION)], local_sem.at[2]
    )
    own_row.start()
    own_grad.start()
    own_weight.start()
    taps[z] = tap_weight[...]

    barrier = pltpu.get_barrier_semaphore()
    partners = [twin]
    partners += [device(dz=step) for step in range(1, PLANES)]
    partners += [device(dx=step) for step in range(1, SIDE)]
    partners += [device(dy=step) for step in range(1, SIDE)]
    for partner in partners:
        pl.semaphore_signal(
            barrier, inc=1, device_id=partner, device_id_type=pl.DeviceIdType.MESH
        )
    pl.semaphore_wait(barrier, len(partners))

    base = core * HALF
    rows_a = pl.ds(pl.multiple_of(base + (y % 2) * QUARTER, QUARTER), QUARTER)
    rows_b = pl.ds(pl.multiple_of(base + (x % 2) * QUARTER, QUARTER), QUARTER)
    other_a = pl.ds(pl.multiple_of(base + (1 - y % 2) * QUARTER, QUARTER), QUARTER)
    other_b = pl.ds(pl.multiple_of(base + (1 - x % 2) * QUARTER, QUARTER), QUARTER)
    start_a, start_b = base + (y % 2) * QUARTER, base + (x % 2) * QUARTER
    part_a = pl.ds(pl.multiple_of(start_a + (x % 2) * EIGHTH, EIGHTH), EIGHTH)
    part_b = pl.ds(pl.multiple_of(start_b + (y % 2) * EIGHTH, EIGHTH), EIGHTH)
    missing_a = pl.ds(pl.multiple_of(start_a + (1 - x % 2) * EIGHTH, EIGHTH), EIGHTH)
    missing_b = pl.ds(pl.multiple_of(start_b + (1 - y % 2) * EIGHTH, EIGHTH), EIGHTH)
    rows_core = pl.ds(pl.multiple_of(base, HALF), HALF)
    rows_twin = pl.ds(pl.multiple_of(HALF - base, HALF), HALF)
    lanes_core, lanes_twin = rows_core, rows_twin

    def pieces(s):
        return (
            weight.at[pl.ds(s * SECTION, SIDE), part_a],
            weight.at[pl.ds(s * SECTION + SIDE, SIDE), part_b],
            taps.at[s, :, :, lanes_core],
        )

    def to_next_plane(direction):
        sources = (
            point_weight.at[pl.ds(0, SIDE), part_a], point_weight.at[pl.ds(SIDE, SIDE), part_b],
            tap_weight.at[:, :, lanes_core],
        )
        at = z if direction == 1 else PLANES
        return [
            remote(source, piece, gz_send.at[at, i], gz_recv.at[z, i], device(dz=direction))
            for i, (source, piece) in enumerate(zip(sources, pieces(z)))
        ]

    def relays(hops, i):
        last = ((0, 2), (1,))
        directions = [d for at, d in enumerate((1, -1)) if hops < 3 or i in last[at]]
        copies = []
        for direction in directions:
            s = (z - direction * hops + PLANES) % PLANES
            piece = pieces(s)[i]
            copies.append(
                remote(piece, piece, gz_send.at[s, i], gz_recv.at[s, i], device(dz=direction))
            )
        return copies

    def arrived(ref, sem):
        pltpu.make_async_copy(ref, ref, sem).wait()

    def along_side(s):
        copies = []
        for low, direction in ((0, 1), (2, -1)):
            piece_a = weight.at[pl.ds(s * SECTION + low, 2), part_a]
            piece_b = weight.at[pl.ds(s * SECTION + SIDE + low, 2), part_b]
            at = low // 2
            copies.append(
                remote(piece_a, piece_a, g1_send.at[s, at, 0], g1_recv.at[s, at, 0], device(dx=direction))
            )
            copies.append(
                remote(piece_b, piece_b, g1_send.at[s, at, 1], g1_recv.at[s, at, 1], device(dy=direction))
            )
        return copies

    def across_side(s):
        copies = []
        for low, direction in ((0, 1), (2, -1)):
            piece_a = weight.at[pl.ds(s * SECTION + low, 2), rows_a]
            piece_b = weight.at[pl.ds(s * SECTION + SIDE + low, 2), rows_b]
            at = low // 2
            copies.append(
                remote(piece_a, piece_a, g2_send.at[s, at, 0], g2_recv.at[s, at, 0], device(dy=direction))
            )
            copies.append(
                remote(piece_b, piece_b, g2_send.at[s, at, 1], g2_recv.at[s, at, 1], device(dx=direction))
            )
        return copies

    def to_twin(s):
        half = weight.at[pl.ds(s * SECTION, SECTION), rows_core]
        lanes = taps.at[s, :, :, lanes_core]
        return (
            remote(half, half, gt_send.at[s, 0], gt_recv.at[s, 0], twin),
            remote(lanes, lanes, gt_send.at[s, 1], gt_recv.at[s, 1], twin),
        )

    for direction in (1, -1):
        for copy in to_next_plane(direction):
            copy.start()

    def forward(s, slot, member, dilation, field):
        live = jnp.where(member < section_cells[s], 1.0, 0.0)
        values = field.astype(jnp.float32)
        before, beyond = neighbours(values, dilation)
        rows = [taps[s, tap, pl.ds(member, 1), :] for tap in range(3)]
        hidden = rows[0] * before + rows[1] * values + rows[2] * beyond
        sigmoid = 0.5 * jnp.tanh(0.5 * hidden) + 0.5
        product = hidden * sigmoid
        activated = (product * live).astype(jnp.bfloat16)
        inputs[slot] = field
        active[slot] = activated
        slope[slot] = (sigmoid + product * (1.0 - sigmoid)) * live
        branch = jnp.dot(activated, weight[slot], preferred_element_type=jnp.float32)
        return (values + branch).astype(jnp.bfloat16)

    own_row.wait()
    x_now[...] = image[...]

    orders, runs = arrival_orders()

    def run_section(s, carry):
        @pl.when(s != z)
        def _():
            arrived(weight.at[pl.ds(s * SECTION, SECTION), rows_twin], gt_recv.at[s, 0])
            arrived(taps.at[s, :, :, lanes_twin], gt_recv.at[s, 1])

        @pl.when(s == z)
        def _():
            own_weight.wait()

        def pair(p, field):
            slot = s * SECTION + 2 * p
            field = forward(s, slot, 2 * p, 1, field)
            return forward(s, slot + 1, 2 * p + 1, 2, field)

        x_now[...] = lax.fori_loop(0, SECTION // 2, pair, x_now[...])
        return carry

    def gather_step(t, carry):
        order, run, done, *seen = carry
        s0 = order % 8
        seen = [s0] + seen
        s1, s2 = seen[LAG_ACROSS], seen[LAG_TWIN]

        for hops, at in enumerate(RING_STEPS, 1):

            @pl.when(t == at)
            def _():
                for i in range(3):
                    for s in {4: (z + hops,)}.get(hops, (z - hops + PLANES, z + hops)):
                        arrived(pieces(s % PLANES)[i], gz_recv.at[s % PLANES, i])
                    if hops < 4:
                        for copy in relays(hops, i):
                            copy.start()

        @pl.when(t < PLANES - 1)
        def _():
            for copy in along_side(s0):
                copy.start()

        @pl.when((t >= LAG_ACROSS) & (t < LAG_ACROSS + PLANES - 1))
        def _():
            for low in (0, 2):
                arrived(weight.at[pl.ds(s1 * SECTION + low, 2), missing_a], g1_recv.at[s1, low // 2, 0])
                arrived(
                    weight.at[pl.ds(s1 * SECTION + SIDE + low, 2), missing_b],
                    g1_recv.at[s1, low // 2, 1],
                )
            for copy in across_side(s1):
                copy.start()

        @pl.when(t >= LAG_TWIN)
        def _():
            for low in (0, 2):
                arrived(weight.at[pl.ds(s2 * SECTION + low, 2), other_a], g2_recv.at[s2, low // 2, 0])
                arrived(
                    weight.at[pl.ds(s2 * SECTION + SIDE + low, 2), other_b],
                    g2_recv.at[s2, low // 2, 1],
                )
            for copy in to_twin(s2):
                copy.start()

        after = done + run % 4
        lax.fori_loop(done, after, run_section, 0)
        return (order // 8, run // 4, after, *seen[:-1])

    start = (by_plane(z, orders), by_plane(z, runs)) + (z * 0,) * (LAG_TWIN + 1)
    done = lax.fori_loop(0, VISITS, gather_step, start)[2]
    lax.fori_loop(done, PLANES, run_section, 0)

    def pair_exchange(s):
        return remote(
            partial.at[s, :, :, 1 - core], from_twin.at[s], rt_send.at[s], rt_recv.at[s], twin
        )

    low, high = pl.ds(0, WIDTH // 2), pl.ds(WIDTH // 2, WIDTH // 2)

    def by_way(s):
        copies = []
        for half, direction in enumerate((1, -1)):
            two = pl.ds(2 * half, 2)
            copies += [
                remote(
                    paired.at[s, (x + 2) % SIDE, two, low], far_a.at[s, half],
                    rf_send.at[s, half, 0], rf_recv.at[s, half, 0], device(dx=direction),
                ),
                remote(
                    paired.at[s, two, (y + 2) % SIDE, high], far_b.at[s, half],
                    rf_send.at[s, half, 1], rf_recv.at[s, half, 1], device(dy=direction),
                ),
            ]
        return copies

    def first_exchange(s):
        copies = []
        for half, direction in enumerate((1, -1)):
            copies += [
                remote(
                    paired.at[s, (x + direction + SIDE) % SIDE, :, low], first_a.at[s, half],
                    r1_send.at[s, half, 0], r1_recv.at[s, half, 0], device(dx=direction),
                ),
                remote(
                    paired.at[s, :, (y + direction + SIDE) % SIDE, high], first_b.at[s, half],
                    r1_send.at[s, half, 1], r1_recv.at[s, half, 1], device(dy=direction),
                ),
            ]
        return copies

    def second_exchange(s, step):
        return (
            remote(
                joined_a.at[s, (y + step) % SIDE], second_a.at[s, step - 1],
                r2_send.at[s, step, 0], r2_recv.at[s, step, 0], device(dy=step),
            ),
            remote(
                joined_b.at[s, (x + step) % SIDE], second_b.at[s, step - 1],
                r2_send.at[s, step, 1], r2_recv.at[s, step, 1], device(dx=step),
            ),
        )

    def to_plane(s):
        return remote(
            square.at[s], planes.at[z], r3_send.at[s], r3_recv.at[z], (s, dp)
        )

    def taps_to_plane(s):
        return remote(
            tap_grads.at[s], tap_planes.at[z], tz_send.at[s], tz_recv.at[z], (s, dp)
        )

    def backward(s, slot, member, dilation, upstream):
        rounded = upstream.astype(jnp.bfloat16)
        grad_active = lax.dot_general(
            rounded, weight[slot], (((1,), (1,)), ((), ())), preferred_element_type=jnp.float32
        )
        grad_hidden = grad_active * slope[slot]
        spread_before, spread_beyond = neighbours(grad_hidden, dilation)
        values = inputs[slot].astype(jnp.float32)
        for tap, spread in enumerate((spread_beyond, grad_hidden, spread_before)):
            tap_grads[s, tap, pl.ds(member, 1), :] = jnp.sum(spread * values, axis=0, keepdims=True)
        grad_matrix = lax.dot_general(
            active[slot], rounded, (((0,), (0,)), ((), ())), preferred_element_type=jnp.float32
        )
        rows = [taps[s, tap, pl.ds(member, 1), :] for tap in range(3)]
        passed = (
            upstream + rows[0] * spread_beyond + rows[1] * grad_hidden + rows[2] * spread_before
        )
        return passed, grad_matrix.reshape(PLANES * SIDE, SECTION, CHANNELS)

    own_grad.wait()
    g_now[...] = grad_row[...].astype(jnp.float32)

    def others(body):
        def visit(s, carry):
            @pl.when(s != z)
            def _():
                body(s)

            return carry

        lax.fori_loop(0, PLANES, visit, 0)

    def tap_side(buffer, place, step, at, **offset):
        return remote(
            buffer.at[place], buffer.at[place], te_send.at[at, step], te_recv.at[at, step],
            device(**offset),
        )

    def tap_swap(buffer, at):
        return remote(buffer.at[core], buffer.at[core], te_send.at[at, 0], te_recv.at[at, 0], twin)

    def tap_cores():
        others(lambda s: arrived(tap_planes.at[s], tz_recv.at[s]))
        total = tap_planes[0]
        for s in range(1, PLANES):
            total += tap_planes[s]
        tap_twin[core] = total
        tap_swap(tap_twin, 0).start()

    def tap_along_x():
        arrived(tap_twin.at[1 - core], te_recv.at[0, 0])
        tap_x[x] = tap_twin[0, :, :, lanes_core] + tap_twin[1, :, :, lanes_core]
        for step in range(1, SIDE):
            tap_side(tap_x, x, step, 1, dx=step).start()

    def tap_along_y():
        for step in range(1, SIDE):
            arrived(tap_x.at[(x + SIDE - step) % SIDE], te_recv.at[1, step])
        tap_y[y] = (tap_x[0] + tap_x[1]) + (tap_x[2] + tap_x[3])
        for step in range(1, SIDE):
            tap_side(tap_y, y, step, 2, dy=step).start()

    def tap_halves():
        for step in range(1, SIDE):
            arrived(tap_y.at[(y + SIDE - step) % SIDE], te_recv.at[2, step])
        tap_final[core] = (tap_y[0] + tap_y[1]) + (tap_y[2] + tap_y[3])
        tap_swap(tap_final, 3).start()

    tap_steps = (tap_cores, tap_along_x, tap_along_y, tap_halves)

    def wide(ref, *index):
        return ref[index].astype(jnp.float32)

    def backward_step(t, carry):
        @pl.when(t < PLANES)
        def _():
            s = PLANES - 1 - t

            def pair(step, upstream):
                p = SECTION // 2 - 1 - step
                slot = s * SECTION + 2 * p
                upstream, odd = backward(s, slot + 1, 2 * p + 1, 2, upstream)
                upstream, even = backward(s, slot, 2 * p, 1, upstream)
                both = jnp.concatenate([even, odd], axis=1).astype(jnp.bfloat16)
                partial[s, :, :, :, pl.ds(pl.multiple_of(16 * p, 16), 16), :] = both.reshape(
                    SIDE, SIDE, 2, 16, CHANNELS
                )
                return upstream

            g_now[...] = lax.fori_loop(0, SECTION // 2, pair, g_now[...])
            pair_exchange(s).start()

            @pl.when(s != z)
            def _():
                taps_to_plane(s).start()

            @pl.when(s == z)
            def _():
                tap_planes[z] = tap_grads[z]

            @pl.when(t != z)
            def _():
                for copy in along_side(t) + across_side(t) + list(to_twin(t)):
                    copy.wait_send()

        s1 = PLANES - 1 - (t - LAG_SUM)

        @pl.when((s1 >= 0) & (s1 < PLANES))
        def _():
            arrived(from_twin.at[s1], rt_recv.at[s1])

            def add(i, carry):
                paired[s1, i] = (wide(partial, s1, i, slice(None), core) + wide(from_twin, s1, i)).astype(
                    jnp.bfloat16
                )
                return carry

            lax.fori_loop(0, SIDE, add, 0)
            for copy in by_way(s1):
                copy.start()

        near = PLANES - 1 - (t - LAG_NEAR)

        @pl.when((near >= 0) & (near < PLANES))
        def _():
            for half, direction in enumerate((1, -1)):
                px, py = (x + direction + SIDE) % SIDE, (y + direction + SIDE) % SIDE
                arrived(far_a.at[near, half], rf_recv.at[near, half, 0])
                arrived(far_b.at[near, half], rf_recv.at[near, half, 1])
                for i in range(2):
                    at = 2 * half + i
                    own_a = paired[near, px, at, : WIDTH // 2, :].astype(jnp.float32)
                    own_b = paired[near, at, py, WIDTH // 2 :, :].astype(jnp.float32)
                    paired[near, px, at, : WIDTH // 2, :] = (
                        own_a + wide(far_a, near, half, i)
                    ).astype(jnp.bfloat16)
                    paired[near, at, py, WIDTH // 2 :, :] = (
                        own_b + wide(far_b, near, half, i)
                    ).astype(jnp.bfloat16)
            for copy in first_exchange(near):
                copy.start()

        s2 = PLANES - 1 - (t - LAG_FIRST)

        @pl.when((s2 >= 0) & (s2 < PLANES))
        def _():
            for half in range(2):
                arrived(first_a.at[s2, half], r1_recv.at[s2, half, 0])
                arrived(first_b.at[s2, half], r1_recv.at[s2, half, 1])
            total_a = paired[s2, x, :, : WIDTH // 2, :].astype(jnp.float32)
            total_b = paired[s2, :, y, WIDTH // 2 :, :].astype(jnp.float32)
            for half in range(2):
                total_a += wide(first_a, s2, half)
                total_b += wide(first_b, s2, half)
            joined_a[s2] = total_a.astype(jnp.bfloat16)
            joined_b[s2] = total_b.astype(jnp.bfloat16)
            for step in range(1, SIDE):
                for copy in second_exchange(s2, step):
                    copy.start()

        s3 = PLANES - 1 - (t - LAG_SECOND)

        @pl.when((s3 >= 0) & (s3 < PLANES))
        def _():
            for step in range(1, SIDE):
                arrived(second_a.at[s3, step - 1], r2_recv.at[s3, step, 0])
                arrived(second_b.at[s3, step - 1], r2_recv.at[s3, step, 1])
            total_a = wide(joined_a, s3, y)
            total_b = wide(joined_b, s3, x)
            for step in range(SIDE - 1):
                total_a += wide(second_a, s3, step)
                total_b += wide(second_b, s3, step)
            total = jnp.concatenate([total_a, total_b], axis=0).astype(jnp.bfloat16)

            @pl.when(s3 != z)
            def _():
                square[s3] = total
                to_plane(s3).start()

            @pl.when(s3 == z)
            def _():
                planes[z] = total

            pair_exchange(s3).wait_send()
            for copy in by_way(s3) + first_exchange(s3):
                copy.wait_send()

        for at, tap_step in enumerate(tap_steps):
            pl.when(t == PLANES + LAG_SECOND - len(tap_steps) + at)(tap_step)

        return carry

    lax.fori_loop(0, PLANES + LAG_SECOND, backward_step, 0)

    for copy in to_next_plane(1) + to_next_plane(-1):
        copy.wait_send()
    for hops in (1, 2, 3):
        for i in range(3):
            for copy in relays(hops, i):
                copy.wait_send()

    def left_sums(s, carry):
        for step in range(1, SIDE):
            for copy in second_exchange(s, step):
                copy.wait_send()
        return carry

    lax.fori_loop(0, PLANES, left_sums, 0)
    tap_swap(tap_twin, 0).wait_send()
    for step in range(1, SIDE):
        tap_side(tap_x, x, step, 1, dx=step).wait_send()
        tap_side(tap_y, y, step, 2, dy=step).wait_send()

    def left_planes(s):
        arrived(planes.at[s], r3_recv.at[s])
        taps_to_plane(s).wait_send()
        to_plane(s).wait_send()

    others(left_planes)
    total = wide(planes, 0)
    for s in range(1, PLANES):
        total += wide(planes, s)
    out_point[...] = total.reshape(SECTION, SECTION, CHANNELS)
    arrived(tap_final.at[1 - core], te_recv.at[3, 0])
    for side in range(2):
        out_taps[:, :, side * HALF : (side + 1) * HALF] = tap_final[side]
    tap_swap(tap_final, 3).wait_send()


def per_device(images, cotangent, section_cells, point_weight, tap_weight):
    cells = PLANES * SECTION
    bf16, f32 = jnp.bfloat16, jnp.float32
    vmem, dma = pltpu.VMEM, pltpu.SemaphoreType.DMA
    hbm_spec = pl.BlockSpec(memory_space=pl.ANY)
    vmem_spec = pl.BlockSpec(memory_space=pltpu.VMEM)
    block = (WIDTH, CHANNELS)
    half_block = (WIDTH // 2, CHANNELS)
    tap_block = (3, SECTION, CHANNELS)
    tap_half = (3, SECTION, HALF)
    scratch = [
        vmem((cells, CHANNELS, CHANNELS), bf16),
        vmem((PLANES,) + tap_block, f32),
        vmem((cells,) + block, bf16),
        vmem((cells,) + block, bf16),
        vmem((cells,) + block, f32),
        vmem(block, bf16),
        vmem(block, bf16),
        vmem(block, bf16),
        vmem(block, f32),
        vmem((PLANES, SIDE, SIDE, 2) + block, bf16),
        vmem((PLANES, SIDE, SIDE) + block, bf16),
        vmem((PLANES, SIDE, SIDE) + block, bf16),
        vmem((PLANES, 2, 2) + half_block, bf16),
        vmem((PLANES, 2, 2) + half_block, bf16),
        vmem((PLANES, 2, SIDE) + half_block, bf16),
        vmem((PLANES, 2, SIDE) + half_block, bf16),
        vmem((PLANES, SIDE) + half_block, bf16),
        vmem((PLANES, SIDE) + half_block, bf16),
        vmem((PLANES, SIDE - 1) + half_block, bf16),
        vmem((PLANES, SIDE - 1) + half_block, bf16),
        vmem((PLANES,) + block, bf16),
        vmem((PLANES,) + block, bf16),
        vmem((PLANES,) + tap_block, f32),
        vmem((PLANES,) + tap_block, f32),
        vmem((2,) + tap_block, f32),
        vmem((SIDE,) + tap_half, f32),
        vmem((SIDE,) + tap_half, f32),
        vmem((2,) + tap_half, f32),
        dma((3,)),
    ]
    for shape in (
        (PLANES + 1, 3), (PLANES, 2, 2), (PLANES, 2, 2), (PLANES, 2),
        (PLANES,), (PLANES, 2, 2), (PLANES, 2, 2), (PLANES, SIDE, 2), (PLANES,),
        (PLANES,), (SIDE, SIDE),
    ):
        scratch += [dma(shape), dma(shape)]
    grad_point, grad_taps = pl.pallas_call(
        window_kernel,
        out_shape=(
            jax.ShapeDtypeStruct((SECTION, SECTION, CHANNELS), f32),
            jax.ShapeDtypeStruct(tap_block, f32),
        ),
        in_specs=[pl.BlockSpec(memory_space=pltpu.SMEM), hbm_spec, hbm_spec, hbm_spec, vmem_spec],
        out_specs=(vmem_spec, vmem_spec),
        scratch_shapes=scratch,
        compiler_params=pltpu.CompilerParams(
            collective_id=0, has_side_effects=True, vmem_limit_bytes=56 << 20
        ),
    )(section_cells, images, cotangent, point_weight, jnp.swapaxes(tap_weight, 0, 1))
    return grad_point, jnp.swapaxes(grad_taps, 0, 1)


def solution(mesh):
    placed = (
        P(None, "dp", None, None),
        P(None, "dp", None, None),
        P(),
        P("segment", None, None),
        P("segment", None, None),
    )
    return jax.shard_map(
        per_device,
        mesh=mesh,
        in_specs=placed,
        out_specs=(P("segment", "dp", None), P("segment", None, None)),
        check_vma=False,
    )
```

```python
import jax
import jax.numpy as jnp
from jax import lax
from jax.experimental import pallas as pl
from jax.experimental.pallas import tpu as pltpu
from jax.sharding import PartitionSpec as P

SECTION = 8
PLANES = 8
SIDE = 4
WIDTH = 64
CHANNELS = 256
HALF = CHANNELS // 2
QUARTER = CHANNELS // 4
EIGHTH = CHANNELS // 8
PIECES = 5
MOST_RUNS = 1
RING_STEPS = (0, 2, 3, 4)
LAG_SUM = 1
LAG_NEAR = 3
LAG_FIRST = 5
LAG_SECOND = 7
LAG_ACROSS = 2
LAG_TWIN = 4
VISITS = PLANES - 1 + LAG_TWIN


def arrival_orders():
    orders, runs = [], []
    for plane in range(PLANES):
        left = [s for s in range(PLANES) if s != plane]
        hops = {s: min((s - plane) % PLANES, (plane - s) % PLANES) for s in left}
        order = []
        while left:
            reach = sum(step <= len(order) for step in RING_STEPS)
            order.append(min(s for s in left if hops[s] <= reach))
            left.remove(order[-1])
        done, counts = 0, []
        for step in range(VISITS):
            count = 0
            while done < PLANES and (done == plane or order.index(done) < step - LAG_TWIN):
                if count == MOST_RUNS:
                    break
                count, done = count + 1, done + 1
            counts.append(count)
        orders.append(sum(s * 8**i for i, s in enumerate(order)))
        runs.append(sum(n * 4**i for i, n in enumerate(counts)))
    return orders, runs


def by_plane(z, values):
    chosen = values[0]
    for plane in range(1, PLANES):
        chosen = jnp.where(z == plane, values[plane], chosen)
    return chosen


def neighbours(values, dilation):
    count = values.shape[0]
    place = lax.broadcasted_iota(jnp.int32, values.shape, 0)
    before = jnp.where(place >= dilation, pltpu.roll(values, dilation, 0), 0.0)
    beyond = jnp.where(place < count - dilation, pltpu.roll(values, count - dilation, 0), 0.0)
    return before, beyond


def window_kernel(
    section_cells, images, cotangent, point_weight, tap_weight,
    out_point, out_taps,
    weight, taps, inputs, active, slope, image, grad_row, x_now, g_now,
    partial, from_twin, paired, far_a, far_b, first_a, first_b, joined_a, joined_b,
    second_a, second_b, square, planes,
    tap_grads, tap_planes, tap_twin, tap_x, tap_y, tap_final,
    local_sem,
    gz_send, gz_recv, g1_send, g1_recv, g2_send, g2_recv, gt_send, gt_recv,
    rt_send, rt_recv, rf_send, rf_recv, r1_send, r1_recv, r2_send, r2_recv, r3_send, r3_recv,
    tz_send, tz_recv, te_send, te_recv,
):
    z = lax.axis_index("segment")
    dp = lax.axis_index("dp")
    x, y, core = dp // 8, (dp // 2) % SIDE, dp % 2

    def device(dz=0, dx=0, dy=0, dc=0):
        px, py = (x + dx + SIDE) % SIDE, (y + dy + SIDE) % SIDE
        return ((z + dz + PLANES) % PLANES, (px * SIDE + py) * 2 + (core + dc) % 2)

    twin = device(dc=1)

    def remote(src, dst, send, recv, target):
        return pltpu.make_async_remote_copy(
            src_ref=src, dst_ref=dst, send_sem=send, recv_sem=recv,
            device_id=target, device_id_type=pl.DeviceIdType.MESH,
        )

    own_row = pltpu.make_async_copy(images.at[z // 2, z % 2], image, local_sem.at[0])
    own_grad = pltpu.make_async_copy(cotangent.at[z // 2, z % 2], grad_row, local_sem.at[1])
    own_weight = pltpu.make_async_copy(
        point_weight, weight.at[pl.ds(z * SECTION, SECTION)], local_sem.at[2]
    )
    own_row.start()
    own_grad.start()
    own_weight.start()
    taps[z] = tap_weight[...]

    barrier = pltpu.get_barrier_semaphore()
    partners = [twin]
    partners += [device(dz=step) for step in range(1, PLANES)]
    partners += [device(dx=step) for step in range(1, SIDE)]
    partners += [device(dy=step) for step in range(1, SIDE)]
    for partner in partners:
        pl.semaphore_signal(
            barrier, inc=1, device_id=partner, device_id_type=pl.DeviceIdType.MESH
        )
    pl.semaphore_wait(barrier, len(partners))

    base = core * HALF
    rows_a = pl.ds(pl.multiple_of(base + (y % 2) * QUARTER, QUARTER), QUARTER)
    rows_b = pl.ds(pl.multiple_of(base + (x % 2) * QUARTER, QUARTER), QUARTER)
    other_a = pl.ds(pl.multiple_of(base + (1 - y % 2) * QUARTER, QUARTER), QUARTER)
    other_b = pl.ds(pl.multiple_of(base + (1 - x % 2) * QUARTER, QUARTER), QUARTER)
    start_a, start_b = base + (y % 2) * QUARTER, base + (x % 2) * QUARTER
    part_a = pl.ds(pl.multiple_of(start_a + (x % 2) * EIGHTH, EIGHTH), EIGHTH)
    part_b = pl.ds(pl.multiple_of(start_b + (y % 2) * EIGHTH, EIGHTH), EIGHTH)
    missing_a = pl.ds(pl.multiple_of(start_a + (1 - x % 2) * EIGHTH, EIGHTH), EIGHTH)
    missing_b = pl.ds(pl.multiple_of(start_b + (1 - y % 2) * EIGHTH, EIGHTH), EIGHTH)
    rows_core = pl.ds(pl.multiple_of(base, HALF), HALF)
    rows_twin = pl.ds(pl.multiple_of(HALF - base, HALF), HALF)
    lanes_core, lanes_twin = rows_core, rows_twin

    def pieces(s):
        return (
            weight.at[pl.ds(s * SECTION, 2), part_a],
            weight.at[pl.ds(s * SECTION + 2, 2), part_a],
            weight.at[pl.ds(s * SECTION + 4, 2), part_b],
            weight.at[pl.ds(s * SECTION + 6, 2), part_b],
            taps.at[s, :, :, lanes_core],
        )

    def to_next_plane(direction):
        sources = (
            point_weight.at[pl.ds(0, 2), part_a], point_weight.at[pl.ds(2, 2), part_a],
            point_weight.at[pl.ds(4, 2), part_b], point_weight.at[pl.ds(6, 2), part_b],
            tap_weight.at[:, :, lanes_core],
        )
        at = z if direction == 1 else PLANES
        return [
            remote(source, piece, gz_send.at[at, i], gz_recv.at[z, i], device(dz=direction))
            for i, (source, piece) in enumerate(zip(sources, pieces(z)))
        ]

    def relays(hops, i):
        last = ((0, 1, 4), (2, 3))
        directions = [d for at, d in enumerate((1, -1)) if hops < 3 or i in last[at]]
        copies = []
        for direction in directions:
            s = (z - direction * hops + PLANES) % PLANES
            piece = pieces(s)[i]
            copies.append(
                remote(piece, piece, gz_send.at[s, i], gz_recv.at[s, i], device(dz=direction))
            )
        return copies

    def arrived(ref, sem):
        pltpu.make_async_copy(ref, ref, sem).wait()

    def along_side(s):
        copies = []
        for low, direction in ((0, 1), (2, -1)):
            piece_a = weight.at[pl.ds(s * SECTION + low, 2), part_a]
            piece_b = weight.at[pl.ds(s * SECTION + SIDE + low, 2), part_b]
            at = low // 2
            copies.append(
                remote(piece_a, piece_a, g1_send.at[s, at, 0], g1_recv.at[s, at, 0], device(dx=direction))
            )
            copies.append(
                remote(piece_b, piece_b, g1_send.at[s, at, 1], g1_recv.at[s, at, 1], device(dy=direction))
            )
        return copies

    def across_side(s):
        copies = []
        for low, direction in ((0, 1), (2, -1)):
            piece_a = weight.at[pl.ds(s * SECTION + low, 2), rows_a]
            piece_b = weight.at[pl.ds(s * SECTION + SIDE + low, 2), rows_b]
            at = low // 2
            copies.append(
                remote(piece_a, piece_a, g2_send.at[s, at, 0], g2_recv.at[s, at, 0], device(dy=direction))
            )
            copies.append(
                remote(piece_b, piece_b, g2_send.at[s, at, 1], g2_recv.at[s, at, 1], device(dx=direction))
            )
        return copies

    def to_twin(s):
        half = weight.at[pl.ds(s * SECTION, SECTION), rows_core]
        lanes = taps.at[s, :, :, lanes_core]
        return (
            remote(half, half, gt_send.at[s, 0], gt_recv.at[s, 0], twin),
            remote(lanes, lanes, gt_send.at[s, 1], gt_recv.at[s, 1], twin),
        )

    for copies in zip(to_next_plane(1), to_next_plane(-1)):
        for copy in copies:
            copy.start()

    def forward(s, slot, member, dilation, field):
        live = jnp.where(member < section_cells[s], 1.0, 0.0)
        values = field.astype(jnp.float32)
        before, beyond = neighbours(values, dilation)
        rows = [taps[s, tap, member : member + 1, :] for tap in range(3)]
        hidden = rows[0] * before + rows[1] * values + rows[2] * beyond
        sigmoid = 0.5 * jnp.tanh(0.5 * hidden) + 0.5
        product = hidden * sigmoid
        activated = (product * live).astype(jnp.bfloat16)
        inputs[slot] = field
        active[slot] = activated
        slope[slot] = (sigmoid + product * (1.0 - sigmoid)) * live
        branch = jnp.dot(activated, weight[slot], preferred_element_type=jnp.float32)
        return (values + branch).astype(jnp.bfloat16)

    own_row.wait()
    x_now[...] = image[...]

    orders, runs = arrival_orders()

    def run_section(s, carry):
        @pl.when(s != z)
        def _():
            arrived(weight.at[pl.ds(s * SECTION, SECTION), rows_twin], gt_recv.at[s, 0])
            arrived(taps.at[s, :, :, lanes_twin], gt_recv.at[s, 1])

        @pl.when(s == z)
        def _():
            own_weight.wait()

        field = x_now[...]
        for member in range(SECTION):
            field = forward(s, s * SECTION + member, member, 1 + member % 2, field)
        x_now[...] = field
        return carry

    def gather_step(t, carry):
        order, run, done, *seen = carry
        s0 = order % 8
        seen = [s0] + seen
        s1, s2 = seen[LAG_ACROSS], seen[LAG_TWIN]

        for hops, at in enumerate(RING_STEPS, 1):

            @pl.when(t == at)
            def _():
                for i in range(PIECES):
                    for s in {4: (z + hops,)}.get(hops, (z - hops + PLANES, z + hops)):
                        arrived(pieces(s % PLANES)[i], gz_recv.at[s % PLANES, i])
                    if hops < 4:
                        for copy in relays(hops, i):
                            copy.start()

        @pl.when(t < PLANES - 1)
        def _():
            for copy in along_side(s0):
                copy.start()

        @pl.when((t >= LAG_ACROSS) & (t < LAG_ACROSS + PLANES - 1))
        def _():
            for low in (0, 2):
                arrived(weight.at[pl.ds(s1 * SECTION + low, 2), missing_a], g1_recv.at[s1, low // 2, 0])
                arrived(
                    weight.at[pl.ds(s1 * SECTION + SIDE + low, 2), missing_b],
                    g1_recv.at[s1, low // 2, 1],
                )
            for copy in across_side(s1):
                copy.start()

        @pl.when(t >= LAG_TWIN)
        def _():
            for low in (0, 2):
                arrived(weight.at[pl.ds(s2 * SECTION + low, 2), other_a], g2_recv.at[s2, low // 2, 0])
                arrived(
                    weight.at[pl.ds(s2 * SECTION + SIDE + low, 2), other_b],
                    g2_recv.at[s2, low // 2, 1],
                )
            for copy in to_twin(s2):
                copy.start()

        after = done + run % 4
        lax.fori_loop(done, after, run_section, 0)
        return (order // 8, run // 4, after, *seen[:-1])

    start = (by_plane(z, orders), by_plane(z, runs)) + (z * 0,) * (LAG_TWIN + 1)
    done = lax.fori_loop(0, VISITS, gather_step, start)[2]
    lax.fori_loop(done, PLANES, run_section, 0)

    def pair_exchange(s):
        return remote(
            partial.at[s, :, :, 1 - core], from_twin.at[s], rt_send.at[s], rt_recv.at[s], twin
        )

    low, high = pl.ds(0, WIDTH // 2), pl.ds(WIDTH // 2, WIDTH // 2)

    def by_way(s):
        copies = []
        for half, direction in enumerate((1, -1)):
            two = pl.ds(2 * half, 2)
            copies += [
                remote(
                    paired.at[s, (x + 2) % SIDE, two, low], far_a.at[s, half],
                    rf_send.at[s, half, 0], rf_recv.at[s, half, 0], device(dx=direction),
                ),
                remote(
                    paired.at[s, two, (y + 2) % SIDE, high], far_b.at[s, half],
                    rf_send.at[s, half, 1], rf_recv.at[s, half, 1], device(dy=direction),
                ),
            ]
        return copies

    def first_exchange(s):
        copies = []
        for half, direction in enumerate((1, -1)):
            copies += [
                remote(
                    paired.at[s, (x + direction + SIDE) % SIDE, :, low], first_a.at[s, half],
                    r1_send.at[s, half, 0], r1_recv.at[s, half, 0], device(dx=direction),
                ),
                remote(
                    paired.at[s, :, (y + direction + SIDE) % SIDE, high], first_b.at[s, half],
                    r1_send.at[s, half, 1], r1_recv.at[s, half, 1], device(dy=direction),
                ),
            ]
        return copies

    def second_exchange(s, step):
        return (
            remote(
                joined_a.at[s, (y + step) % SIDE], second_a.at[s, step - 1],
                r2_send.at[s, step, 0], r2_recv.at[s, step, 0], device(dy=step),
            ),
            remote(
                joined_b.at[s, (x + step) % SIDE], second_b.at[s, step - 1],
                r2_send.at[s, step, 1], r2_recv.at[s, step, 1], device(dx=step),
            ),
        )

    def to_plane(s):
        return remote(
            square.at[s], planes.at[z], r3_send.at[s], r3_recv.at[z], (s, dp)
        )

    def taps_to_plane(s):
        return remote(
            tap_grads.at[s], tap_planes.at[z], tz_send.at[s], tz_recv.at[z], (s, dp)
        )

    def backward(s, slot, member, dilation, upstream):
        rounded = upstream.astype(jnp.bfloat16)
        grad_active = lax.dot_general(
            rounded, weight[slot], (((1,), (1,)), ((), ())), preferred_element_type=jnp.float32
        )
        grad_hidden = grad_active * slope[slot]
        spread_before, spread_beyond = neighbours(grad_hidden, dilation)
        values = inputs[slot].astype(jnp.float32)
        for tap, spread in enumerate((spread_beyond, grad_hidden, spread_before)):
            tap_grads[s, tap, member : member + 1, :] = jnp.sum(spread * values, axis=0, keepdims=True)
        grad_matrix = lax.dot_general(
            active[slot], rounded, (((0,), (0,)), ((), ())), preferred_element_type=jnp.float32
        )
        rows = [taps[s, tap, member : member + 1, :] for tap in range(3)]
        passed = (
            upstream + rows[0] * spread_beyond + rows[1] * grad_hidden + rows[2] * spread_before
        )
        return passed, grad_matrix.reshape(PLANES * SIDE, SECTION, CHANNELS)

    own_grad.wait()
    g_now[...] = grad_row[...].astype(jnp.float32)

    def others(body):
        def visit(s, carry):
            @pl.when(s != z)
            def _():
                body(s)

            return carry

        lax.fori_loop(0, PLANES, visit, 0)

    def tap_side(buffer, place, step, at, **offset):
        return remote(
            buffer.at[place], buffer.at[place], te_send.at[at, step], te_recv.at[at, step],
            device(**offset),
        )

    def tap_swap(buffer, at):
        return remote(buffer.at[core], buffer.at[core], te_send.at[at, 0], te_recv.at[at, 0], twin)

    def tap_cores():
        others(lambda s: arrived(tap_planes.at[s], tz_recv.at[s]))
        total = tap_planes[0]
        for s in range(1, PLANES):
            total += tap_planes[s]
        tap_twin[core] = total
        tap_swap(tap_twin, 0).start()

    def tap_along_x():
        arrived(tap_twin.at[1 - core], te_recv.at[0, 0])
        tap_x[x] = tap_twin[0, :, :, lanes_core] + tap_twin[1, :, :, lanes_core]
        for step in range(1, SIDE):
            tap_side(tap_x, x, step, 1, dx=step).start()

    def tap_along_y():
        for step in range(1, SIDE):
            arrived(tap_x.at[(x + SIDE - step) % SIDE], te_recv.at[1, step])
        tap_y[y] = (tap_x[0] + tap_x[1]) + (tap_x[2] + tap_x[3])
        for step in range(1, SIDE):
            tap_side(tap_y, y, step, 2, dy=step).start()

    def tap_halves():
        for step in range(1, SIDE):
            arrived(tap_y.at[(y + SIDE - step) % SIDE], te_recv.at[2, step])
        tap_final[core] = (tap_y[0] + tap_y[1]) + (tap_y[2] + tap_y[3])
        tap_swap(tap_final, 3).start()

    tap_steps = (tap_cores, tap_along_x, tap_along_y, tap_halves)

    def wide(ref, *index):
        return ref[index].astype(jnp.float32)

    def backward_step(t, carry):
        @pl.when(t < PLANES)
        def _():
            s = PLANES - 1 - t

            upstream = g_now[...]
            for p in reversed(range(SECTION // 2)):
                slot = s * SECTION + 2 * p
                upstream, odd = backward(s, slot + 1, 2 * p + 1, 2, upstream)
                upstream, even = backward(s, slot, 2 * p, 1, upstream)
                both = jnp.concatenate([even, odd], axis=1).astype(jnp.bfloat16)
                partial[s, :, :, :, 16 * p : 16 * p + 16, :] = both.reshape(
                    SIDE, SIDE, 2, 16, CHANNELS
                )
            g_now[...] = upstream
            pair_exchange(s).start()

            @pl.when(s != z)
            def _():
                taps_to_plane(s).start()

            @pl.when(s == z)
            def _():
                tap_planes[z] = tap_grads[z]

            @pl.when(t != z)
            def _():
                for copy in along_side(t) + across_side(t) + list(to_twin(t)):
                    copy.wait_send()

        s1 = PLANES - 1 - (t - LAG_SUM)

        @pl.when((s1 >= 0) & (s1 < PLANES))
        def _():
            arrived(from_twin.at[s1], rt_recv.at[s1])

            def add(i, carry):
                paired[s1, i] = (wide(partial, s1, i, slice(None), core) + wide(from_twin, s1, i)).astype(
                    jnp.bfloat16
                )
                return carry

            lax.fori_loop(0, SIDE, add, 0)
            for copy in by_way(s1):
                copy.start()

        near = PLANES - 1 - (t - LAG_NEAR)

        @pl.when((near >= 0) & (near < PLANES))
        def _():
            for half, direction in enumerate((1, -1)):
                px, py = (x + direction + SIDE) % SIDE, (y + direction + SIDE) % SIDE
                arrived(far_a.at[near, half], rf_recv.at[near, half, 0])
                arrived(far_b.at[near, half], rf_recv.at[near, half, 1])
                for i in range(2):
                    at = 2 * half + i
                    own_a = paired[near, px, at, : WIDTH // 2, :].astype(jnp.float32)
                    own_b = paired[near, at, py, WIDTH // 2 :, :].astype(jnp.float32)
                    paired[near, px, at, : WIDTH // 2, :] = (
                        own_a + wide(far_a, near, half, i)
                    ).astype(jnp.bfloat16)
                    paired[near, at, py, WIDTH // 2 :, :] = (
                        own_b + wide(far_b, near, half, i)
                    ).astype(jnp.bfloat16)
            for copy in first_exchange(near):
                copy.start()

        s2 = PLANES - 1 - (t - LAG_FIRST)

        @pl.when((s2 >= 0) & (s2 < PLANES))
        def _():
            for half in range(2):
                arrived(first_a.at[s2, half], r1_recv.at[s2, half, 0])
                arrived(first_b.at[s2, half], r1_recv.at[s2, half, 1])
            total_a = paired[s2, x, :, : WIDTH // 2, :].astype(jnp.float32)
            total_b = paired[s2, :, y, WIDTH // 2 :, :].astype(jnp.float32)
            for half in range(2):
                total_a += wide(first_a, s2, half)
                total_b += wide(first_b, s2, half)
            joined_a[s2] = total_a.astype(jnp.bfloat16)
            joined_b[s2] = total_b.astype(jnp.bfloat16)
            for step in range(1, SIDE):
                for copy in second_exchange(s2, step):
                    copy.start()

        s3 = PLANES - 1 - (t - LAG_SECOND)

        @pl.when((s3 >= 0) & (s3 < PLANES))
        def _():
            for step in range(1, SIDE):
                arrived(second_a.at[s3, step - 1], r2_recv.at[s3, step, 0])
                arrived(second_b.at[s3, step - 1], r2_recv.at[s3, step, 1])
            total_a = wide(joined_a, s3, y)
            total_b = wide(joined_b, s3, x)
            for step in range(SIDE - 1):
                total_a += wide(second_a, s3, step)
                total_b += wide(second_b, s3, step)
            total = jnp.concatenate([total_a, total_b], axis=0).astype(jnp.bfloat16)

            @pl.when(s3 != z)
            def _():
                square[s3] = total
                to_plane(s3).start()

            @pl.when(s3 == z)
            def _():
                planes[z] = total

            pair_exchange(s3).wait_send()
            for copy in by_way(s3) + first_exchange(s3):
                copy.wait_send()

        for at, tap_step in enumerate(tap_steps):
            pl.when(t == PLANES + LAG_SECOND - len(tap_steps) + at)(tap_step)

        return carry

    lax.fori_loop(0, PLANES + LAG_SECOND, backward_step, 0)

    for copy in to_next_plane(1) + to_next_plane(-1):
        copy.wait_send()
    for hops in (1, 2, 3):
        for i in range(PIECES):
            for copy in relays(hops, i):
                copy.wait_send()

    def left_sums(s, carry):
        for step in range(1, SIDE):
            for copy in second_exchange(s, step):
                copy.wait_send()
        return carry

    lax.fori_loop(0, PLANES, left_sums, 0)
    tap_swap(tap_twin, 0).wait_send()
    for step in range(1, SIDE):
        tap_side(tap_x, x, step, 1, dx=step).wait_send()
        tap_side(tap_y, y, step, 2, dy=step).wait_send()

    def left_planes(s):
        arrived(planes.at[s], r3_recv.at[s])
        taps_to_plane(s).wait_send()
        to_plane(s).wait_send()

    others(left_planes)
    total = wide(planes, 0)
    for s in range(1, PLANES):
        total += wide(planes, s)
    out_point[...] = total.reshape(SECTION, SECTION, CHANNELS)
    arrived(tap_final.at[1 - core], te_recv.at[3, 0])
    for side in range(2):
        out_taps[:, :, side * HALF : (side + 1) * HALF] = tap_final[side]
    tap_swap(tap_final, 3).wait_send()


def per_device(images, cotangent, section_cells, point_weight, tap_weight):
    cells = PLANES * SECTION
    bf16, f32 = jnp.bfloat16, jnp.float32
    vmem, dma = pltpu.VMEM, pltpu.SemaphoreType.DMA
    hbm_spec = pl.BlockSpec(memory_space=pl.ANY)
    vmem_spec = pl.BlockSpec(memory_space=pltpu.VMEM)
    block = (WIDTH, CHANNELS)
    half_block = (WIDTH // 2, CHANNELS)
    tap_block = (3, SECTION, CHANNELS)
    tap_half = (3, SECTION, HALF)
    scratch = [
        vmem((cells, CHANNELS, CHANNELS), bf16),
        vmem((PLANES,) + tap_block, f32),
        vmem((cells,) + block, bf16),
        vmem((cells,) + block, bf16),
        vmem((cells,) + block, f32),
        vmem(block, bf16),
        vmem(block, bf16),
        vmem(block, bf16),
        vmem(block, f32),
        vmem((PLANES, SIDE, SIDE, 2) + block, bf16),
        vmem((PLANES, SIDE, SIDE) + block, bf16),
        vmem((PLANES, SIDE, SIDE) + block, bf16),
        vmem((PLANES, 2, 2) + half_block, bf16),
        vmem((PLANES, 2, 2) + half_block, bf16),
        vmem((PLANES, 2, SIDE) + half_block, bf16),
        vmem((PLANES, 2, SIDE) + half_block, bf16),
        vmem((PLANES, SIDE) + half_block, bf16),
        vmem((PLANES, SIDE) + half_block, bf16),
        vmem((PLANES, SIDE - 1) + half_block, bf16),
        vmem((PLANES, SIDE - 1) + half_block, bf16),
        vmem((PLANES,) + block, bf16),
        vmem((PLANES,) + block, bf16),
        vmem((PLANES,) + tap_block, f32),
        vmem((PLANES,) + tap_block, f32),
        vmem((2,) + tap_block, f32),
        vmem((SIDE,) + tap_half, f32),
        vmem((SIDE,) + tap_half, f32),
        vmem((2,) + tap_half, f32),
        dma((3,)),
    ]
    for shape in (
        (PLANES + 1, PIECES), (PLANES, 2, 2), (PLANES, 2, 2), (PLANES, 2),
        (PLANES,), (PLANES, 2, 2), (PLANES, 2, 2), (PLANES, SIDE, 2), (PLANES,),
        (PLANES,), (SIDE, SIDE),
    ):
        scratch += [dma(shape), dma(shape)]
    grad_point, grad_taps = pl.pallas_call(
        window_kernel,
        out_shape=(
            jax.ShapeDtypeStruct((SECTION, SECTION, CHANNELS), f32),
            jax.ShapeDtypeStruct(tap_block, f32),
        ),
        in_specs=[pl.BlockSpec(memory_space=pltpu.SMEM), hbm_spec, hbm_spec, hbm_spec, vmem_spec],
        out_specs=(vmem_spec, vmem_spec),
        scratch_shapes=scratch,
        compiler_params=pltpu.CompilerParams(
            collective_id=0, has_side_effects=True, vmem_limit_bytes=56 << 20
        ),
    )(section_cells, images, cotangent, point_weight, jnp.swapaxes(tap_weight, 0, 1))
    return grad_point, jnp.swapaxes(grad_taps, 0, 1)


def solution(mesh):
    placed = (
        P(None, "dp", None, None),
        P(None, "dp", None, None),
        P(),
        P("segment", None, None),
        P("segment", None, None),
    )
    return jax.shard_map(
        per_device,
        mesh=mesh,
        in_specs=placed,
        out_specs=(P("segment", "dp", None), P("segment", None, None)),
        check_vma=False,
    )
```

```python
import jax
import jax.numpy as jnp
from jax import lax
from jax.experimental import pallas as pl
from jax.experimental.pallas import tpu as pltpu
from jax.sharding import PartitionSpec as P

SECTION = 8
PLANES = 8
SIDE = 4
WIDTH = 64
CHANNELS = 256
HALF = CHANNELS // 2
QUARTER = CHANNELS // 4
EIGHTH = CHANNELS // 8
PIECES = 5
MOST_RUNS = 2
RING_STEPS = (0, 2, 3, 4)
LAG_SUM = 1
LAG_NEAR = 3
LAG_FIRST = 5
LAG_SECOND = 7
LAG_ACROSS = 2
LAG_TWIN = 4
VISITS = PLANES - 1 + LAG_TWIN


def arrival_orders():
    orders, runs = [], []
    for plane in range(PLANES):
        left = [s for s in range(PLANES) if s != plane]
        hops = {s: min((s - plane) % PLANES, (plane - s) % PLANES) for s in left}
        order = []
        while left:
            reach = sum(step <= len(order) for step in RING_STEPS)
            order.append(min(s for s in left if hops[s] <= reach))
            left.remove(order[-1])
        done, counts = 0, []
        for step in range(VISITS):
            count = 0
            while done < PLANES and (done == plane or order.index(done) < step - LAG_TWIN):
                if count == MOST_RUNS:
                    break
                count, done = count + 1, done + 1
            counts.append(count)
        orders.append(sum(s * 8**i for i, s in enumerate(order)))
        runs.append(sum(n * 4**i for i, n in enumerate(counts)))
    return orders, runs


def by_plane(z, values):
    chosen = values[0]
    for plane in range(1, PLANES):
        chosen = jnp.where(z == plane, values[plane], chosen)
    return chosen


def neighbours(values, dilation):
    count = values.shape[0]
    place = lax.broadcasted_iota(jnp.int32, values.shape, 0)
    before = jnp.where(place >= dilation, pltpu.roll(values, dilation, 0), 0.0)
    beyond = jnp.where(place < count - dilation, pltpu.roll(values, count - dilation, 0), 0.0)
    return before, beyond


def window_kernel(
    section_cells, images, cotangent, point_weight, tap_weight,
    out_point, out_taps,
    weight, taps, inputs, active, slope, image, grad_row, x_now, g_now,
    partial, from_twin, paired, far_a, far_b, first_a, first_b, joined_a, joined_b,
    second_a, second_b, square, planes,
    tap_grads, tap_planes, tap_twin, tap_x, tap_y, tap_final,
    local_sem,
    gz_send, gz_recv, g1_send, g1_recv, g2_send, g2_recv, gt_send, gt_recv,
    rt_send, rt_recv, rf_send, rf_recv, r1_send, r1_recv, r2_send, r2_recv, r3_send, r3_recv,
    tz_send, tz_recv, te_send, te_recv,
):
    z = lax.axis_index("segment")
    dp = lax.axis_index("dp")
    x, y, core = dp // 8, (dp // 2) % SIDE, dp % 2

    def device(dz=0, dx=0, dy=0, dc=0):
        px, py = (x + dx + SIDE) % SIDE, (y + dy + SIDE) % SIDE
        return ((z + dz + PLANES) % PLANES, (px * SIDE + py) * 2 + (core + dc) % 2)

    twin = device(dc=1)

    def remote(src, dst, send, recv, target):
        return pltpu.make_async_remote_copy(
            src_ref=src, dst_ref=dst, send_sem=send, recv_sem=recv,
            device_id=target, device_id_type=pl.DeviceIdType.MESH,
        )

    own_row = pltpu.make_async_copy(images.at[z // 2, z % 2], image, local_sem.at[0])
    own_grad = pltpu.make_async_copy(cotangent.at[z // 2, z % 2], grad_row, local_sem.at[1])
    own_weight = pltpu.make_async_copy(
        point_weight, weight.at[pl.ds(z * SECTION, SECTION)], local_sem.at[2]
    )
    own_row.start()
    own_grad.start()
    own_weight.start()
    taps[z] = tap_weight[...]

    barrier = pltpu.get_barrier_semaphore()
    partners = [twin]
    partners += [device(dz=step) for step in range(1, PLANES)]
    partners += [device(dx=step) for step in range(1, SIDE)]
    partners += [device(dy=step) for step in range(1, SIDE)]
    for partner in partners:
        pl.semaphore_signal(
            barrier, inc=1, device_id=partner, device_id_type=pl.DeviceIdType.MESH
        )
    pl.semaphore_wait(barrier, len(partners))

    base = core * HALF
    rows_a = pl.ds(pl.multiple_of(base + (y % 2) * QUARTER, QUARTER), QUARTER)
    rows_b = pl.ds(pl.multiple_of(base + (x % 2) * QUARTER, QUARTER), QUARTER)
    other_a = pl.ds(pl.multiple_of(base + (1 - y % 2) * QUARTER, QUARTER), QUARTER)
    other_b = pl.ds(pl.multiple_of(base + (1 - x % 2) * QUARTER, QUARTER), QUARTER)
    start_a, start_b = base + (y % 2) * QUARTER, base + (x % 2) * QUARTER
    part_a = pl.ds(pl.multiple_of(start_a + (x % 2) * EIGHTH, EIGHTH), EIGHTH)
    part_b = pl.ds(pl.multiple_of(start_b + (y % 2) * EIGHTH, EIGHTH), EIGHTH)
    missing_a = pl.ds(pl.multiple_of(start_a + (1 - x % 2) * EIGHTH, EIGHTH), EIGHTH)
    missing_b = pl.ds(pl.multiple_of(start_b + (1 - y % 2) * EIGHTH, EIGHTH), EIGHTH)
    rows_core = pl.ds(pl.multiple_of(base, HALF), HALF)
    rows_twin = pl.ds(pl.multiple_of(HALF - base, HALF), HALF)
    lanes_core, lanes_twin = rows_core, rows_twin

    def pieces(s):
        return (
            weight.at[pl.ds(s * SECTION, 2), part_a],
            weight.at[pl.ds(s * SECTION + 2, 2), part_a],
            weight.at[pl.ds(s * SECTION + 4, 2), part_b],
            weight.at[pl.ds(s * SECTION + 6, 2), part_b],
            taps.at[s, :, :, lanes_core],
        )

    def to_next_plane(direction):
        sources = (
            point_weight.at[pl.ds(0, 2), part_a], point_weight.at[pl.ds(2, 2), part_a],
            point_weight.at[pl.ds(4, 2), part_b], point_weight.at[pl.ds(6, 2), part_b],
            tap_weight.at[:, :, lanes_core],
        )
        at = z if direction == 1 else PLANES
        return [
            remote(source, piece, gz_send.at[at, i], gz_recv.at[z, i], device(dz=direction))
            for i, (source, piece) in enumerate(zip(sources, pieces(z)))
        ]

    def relays(hops, i):
        last = ((0, 1, 4), (2, 3))
        directions = [d for at, d in enumerate((1, -1)) if hops < 3 or i in last[at]]
        copies = []
        for direction in directions:
            s = (z - direction * hops + PLANES) % PLANES
            piece = pieces(s)[i]
            copies.append(
                remote(piece, piece, gz_send.at[s, i], gz_recv.at[s, i], device(dz=direction))
            )
        return copies

    def arrived(ref, sem):
        pltpu.make_async_copy(ref, ref, sem).wait()

    def along_side(s):
        copies = []
        for low, direction in ((0, 1), (2, -1)):
            piece_a = weight.at[pl.ds(s * SECTION + low, 2), part_a]
            piece_b = weight.at[pl.ds(s * SECTION + SIDE + low, 2), part_b]
            at = low // 2
            copies.append(
                remote(piece_a, piece_a, g1_send.at[s, at, 0], g1_recv.at[s, at, 0], device(dx=direction))
            )
            copies.append(
                remote(piece_b, piece_b, g1_send.at[s, at, 1], g1_recv.at[s, at, 1], device(dy=direction))
            )
        return copies

    def across_side(s):
        copies = []
        for low, direction in ((0, 1), (2, -1)):
            piece_a = weight.at[pl.ds(s * SECTION + low, 2), rows_a]
            piece_b = weight.at[pl.ds(s * SECTION + SIDE + low, 2), rows_b]
            at = low // 2
            copies.append(
                remote(piece_a, piece_a, g2_send.at[s, at, 0], g2_recv.at[s, at, 0], device(dy=direction))
            )
            copies.append(
                remote(piece_b, piece_b, g2_send.at[s, at, 1], g2_recv.at[s, at, 1], device(dx=direction))
            )
        return copies

    def to_twin(s):
        half = weight.at[pl.ds(s * SECTION, SECTION), rows_core]
        lanes = taps.at[s, :, :, lanes_core]
        return (
            remote(half, half, gt_send.at[s, 0], gt_recv.at[s, 0], twin),
            remote(lanes, lanes, gt_send.at[s, 1], gt_recv.at[s, 1], twin),
        )

    for copies in zip(to_next_plane(1), to_next_plane(-1)):
        for copy in copies:
            copy.start()

    def forward(s, slot, member, dilation, field):
        values = field.astype(jnp.float32)
        live = jnp.full(values.shape, section_cells[s]) > member
        before, beyond = neighbours(values, dilation)
        rows = [taps[s, tap, member : member + 1, :] for tap in range(3)]
        hidden = rows[0] * before + rows[1] * values + rows[2] * beyond
        sigmoid = 0.5 * jnp.tanh(0.5 * hidden) + 0.5
        product = hidden * sigmoid
        activated = jnp.where(live, product, 0.0).astype(jnp.bfloat16)
        inputs[slot] = field
        active[slot] = activated
        slope[slot] = jnp.where(live, sigmoid + product * (1.0 - sigmoid), 0.0)
        branch = jnp.dot(activated, weight[slot], preferred_element_type=jnp.float32)
        return (values + branch).astype(jnp.bfloat16)

    own_row.wait()
    x_now[...] = image[...]

    orders, runs = arrival_orders()

    def run_section(s, carry):
        @pl.when(s != z)
        def _():
            arrived(weight.at[pl.ds(s * SECTION, SECTION), rows_twin], gt_recv.at[s, 0])
            arrived(taps.at[s, :, :, lanes_twin], gt_recv.at[s, 1])

        @pl.when(s == z)
        def _():
            own_weight.wait()

        field = x_now[...]
        for member in range(SECTION):
            field = forward(s, s * SECTION + member, member, 1 + member % 2, field)
        x_now[...] = field
        return carry

    def gather_step(t, carry):
        order, run, done, *seen = carry
        s0 = order % 8
        seen = [s0] + seen
        s1, s2 = seen[LAG_ACROSS], seen[LAG_TWIN]

        for hops, at in enumerate(RING_STEPS, 1):

            @pl.when(t == at)
            def _():
                for i in range(PIECES):
                    for s in {4: (z + hops,)}.get(hops, (z - hops + PLANES, z + hops)):
                        arrived(pieces(s % PLANES)[i], gz_recv.at[s % PLANES, i])
                    if hops < 4:
                        for copy in relays(hops, i):
                            copy.start()

        @pl.when(t < PLANES - 1)
        def _():
            for copy in along_side(s0):
                copy.start()

        @pl.when((t >= LAG_ACROSS) & (t < LAG_ACROSS + PLANES - 1))
        def _():
            for low in (0, 2):
                arrived(weight.at[pl.ds(s1 * SECTION + low, 2), missing_a], g1_recv.at[s1, low // 2, 0])
                arrived(
                    weight.at[pl.ds(s1 * SECTION + SIDE + low, 2), missing_b],
                    g1_recv.at[s1, low // 2, 1],
                )
            for copy in across_side(s1):
                copy.start()

        @pl.when(t >= LAG_TWIN)
        def _():
            for low in (0, 2):
                arrived(weight.at[pl.ds(s2 * SECTION + low, 2), other_a], g2_recv.at[s2, low // 2, 0])
                arrived(
                    weight.at[pl.ds(s2 * SECTION + SIDE + low, 2), other_b],
                    g2_recv.at[s2, low // 2, 1],
                )
            for copy in to_twin(s2):
                copy.start()

        after = done + run % 4
        lax.fori_loop(done, after, run_section, 0)
        return (order // 8, run // 4, after, *seen[:-1])

    start = (by_plane(z, orders), by_plane(z, runs)) + (z * 0,) * (LAG_TWIN + 1)
    done = lax.fori_loop(0, VISITS, gather_step, start)[2]
    lax.fori_loop(done, PLANES, run_section, 0)

    def pair_exchange(s):
        return remote(
            partial.at[s, :, :, 1 - core], from_twin.at[s], rt_send.at[s], rt_recv.at[s], twin
        )

    low, high = pl.ds(0, WIDTH // 2), pl.ds(WIDTH // 2, WIDTH // 2)

    def by_way(s):
        copies = []
        for half, direction in enumerate((1, -1)):
            two = pl.ds(2 * half, 2)
            copies += [
                remote(
                    paired.at[s, (x + 2) % SIDE, two, low], far_a.at[s, half],
                    rf_send.at[s, half, 0], rf_recv.at[s, half, 0], device(dx=direction),
                ),
                remote(
                    paired.at[s, two, (y + 2) % SIDE, high], far_b.at[s, half],
                    rf_send.at[s, half, 1], rf_recv.at[s, half, 1], device(dy=direction),
                ),
            ]
        return copies

    def first_exchange(s):
        copies = []
        for half, direction in enumerate((1, -1)):
            copies += [
                remote(
                    paired.at[s, (x + direction + SIDE) % SIDE, :, low], first_a.at[s, half],
                    r1_send.at[s, half, 0], r1_recv.at[s, half, 0], device(dx=direction),
                ),
                remote(
                    paired.at[s, :, (y + direction + SIDE) % SIDE, high], first_b.at[s, half],
                    r1_send.at[s, half, 1], r1_recv.at[s, half, 1], device(dy=direction),
                ),
            ]
        return copies

    def second_exchange(s, step):
        return (
            remote(
                joined_a.at[s, (y + step) % SIDE], second_a.at[s, step - 1],
                r2_send.at[s, step, 0], r2_recv.at[s, step, 0], device(dy=step),
            ),
            remote(
                joined_b.at[s, (x + step) % SIDE], second_b.at[s, step - 1],
                r2_send.at[s, step, 1], r2_recv.at[s, step, 1], device(dx=step),
            ),
        )

    def to_plane(s):
        return remote(
            square.at[s], planes.at[z], r3_send.at[s], r3_recv.at[z], (s, dp)
        )

    def taps_to_plane(s):
        return remote(
            tap_grads.at[s], tap_planes.at[z], tz_send.at[s], tz_recv.at[z], (s, dp)
        )

    def backward(s, slot, member, dilation, upstream):
        rounded = upstream.astype(jnp.bfloat16)
        grad_active = lax.dot_general(
            rounded, weight[slot], (((1,), (1,)), ((), ())), preferred_element_type=jnp.float32
        )
        live = jnp.full(grad_active.shape, section_cells[s]) > member
        grad_hidden = jnp.where(live, grad_active * slope[slot], 0.0)
        spread_before, spread_beyond = neighbours(grad_hidden, dilation)
        values = inputs[slot].astype(jnp.float32)
        for tap, spread in enumerate((spread_beyond, grad_hidden, spread_before)):
            tap_grads[s, tap, member : member + 1, :] = jnp.sum(spread * values, axis=0, keepdims=True)
        grad_matrix = lax.dot_general(
            active[slot], rounded, (((0,), (0,)), ((), ())), preferred_element_type=jnp.float32
        )
        rows = [taps[s, tap, member : member + 1, :] for tap in range(3)]
        passed = (
            upstream + rows[0] * spread_beyond + rows[1] * grad_hidden + rows[2] * spread_before
        )
        return passed, grad_matrix.reshape(PLANES * SIDE, SECTION, CHANNELS)

    own_grad.wait()
    g_now[...] = grad_row[...].astype(jnp.float32)

    def others(body):
        def visit(s, carry):
            @pl.when(s != z)
            def _():
                body(s)

            return carry

        lax.fori_loop(0, PLANES, visit, 0)

    def tap_side(buffer, place, step, at, **offset):
        return remote(
            buffer.at[place], buffer.at[place], te_send.at[at, step], te_recv.at[at, step],
            device(**offset),
        )

    def tap_swap(buffer, at):
        return remote(buffer.at[core], buffer.at[core], te_send.at[at, 0], te_recv.at[at, 0], twin)

    def tap_cores():
        others(lambda s: arrived(tap_planes.at[s], tz_recv.at[s]))
        total = tap_planes[0]
        for s in range(1, PLANES):
            total += tap_planes[s]
        tap_twin[core] = total
        tap_swap(tap_twin, 0).start()

    def tap_along_x():
        arrived(tap_twin.at[1 - core], te_recv.at[0, 0])
        tap_x[x] = tap_twin[0, :, :, lanes_core] + tap_twin[1, :, :, lanes_core]
        for step in range(1, SIDE):
            tap_side(tap_x, x, step, 1, dx=step).start()

    def tap_along_y():
        for step in range(1, SIDE):
            arrived(tap_x.at[(x + SIDE - step) % SIDE], te_recv.at[1, step])
        tap_y[y] = (tap_x[0] + tap_x[1]) + (tap_x[2] + tap_x[3])
        for step in range(1, SIDE):
            tap_side(tap_y, y, step, 2, dy=step).start()

    def tap_halves():
        for step in range(1, SIDE):
            arrived(tap_y.at[(y + SIDE - step) % SIDE], te_recv.at[2, step])
        tap_final[core] = (tap_y[0] + tap_y[1]) + (tap_y[2] + tap_y[3])
        tap_swap(tap_final, 3).start()

    tap_steps = (tap_cores, tap_along_x, tap_along_y, tap_halves)

    def wide(ref, *index):
        return ref[index].astype(jnp.float32)

    def backward_step(t, carry):
        @pl.when(t < PLANES)
        def _():
            s = PLANES - 1 - t

            upstream = g_now[...]
            for p in reversed(range(SECTION // 2)):
                slot = s * SECTION + 2 * p
                upstream, odd = backward(s, slot + 1, 2 * p + 1, 2, upstream)
                upstream, even = backward(s, slot, 2 * p, 1, upstream)
                both = jnp.concatenate([even, odd], axis=1).astype(jnp.bfloat16)
                partial[s, :, :, :, 16 * p : 16 * p + 16, :] = both.reshape(
                    SIDE, SIDE, 2, 16, CHANNELS
                )
            g_now[...] = upstream
            pair_exchange(s).start()

            @pl.when(s != z)
            def _():
                taps_to_plane(s).start()

            @pl.when(s == z)
            def _():
                tap_planes[z] = tap_grads[z]

            @pl.when(t != z)
            def _():
                for copy in along_side(t) + across_side(t) + list(to_twin(t)):
                    copy.wait_send()

        s1 = PLANES - 1 - (t - LAG_SUM)

        @pl.when((s1 >= 0) & (s1 < PLANES))
        def _():
            arrived(from_twin.at[s1], rt_recv.at[s1])

            def add(i, carry):
                paired[s1, i] = (wide(partial, s1, i, slice(None), core) + wide(from_twin, s1, i)).astype(
                    jnp.bfloat16
                )
                return carry

            lax.fori_loop(0, SIDE, add, 0)
            for copy in by_way(s1):
                copy.start()

        near = PLANES - 1 - (t - LAG_NEAR)

        @pl.when((near >= 0) & (near < PLANES))
        def _():
            for half, direction in enumerate((1, -1)):
                px, py = (x + direction + SIDE) % SIDE, (y + direction + SIDE) % SIDE
                arrived(far_a.at[near, half], rf_recv.at[near, half, 0])
                arrived(far_b.at[near, half], rf_recv.at[near, half, 1])
                for i in range(2):
                    at = 2 * half + i
                    own_a = paired[near, px, at, : WIDTH // 2, :].astype(jnp.float32)
                    own_b = paired[near, at, py, WIDTH // 2 :, :].astype(jnp.float32)
                    paired[near, px, at, : WIDTH // 2, :] = (
                        own_a + wide(far_a, near, half, i)
                    ).astype(jnp.bfloat16)
                    paired[near, at, py, WIDTH // 2 :, :] = (
                        own_b + wide(far_b, near, half, i)
                    ).astype(jnp.bfloat16)
            for copy in first_exchange(near):
                copy.start()

        s2 = PLANES - 1 - (t - LAG_FIRST)

        @pl.when((s2 >= 0) & (s2 < PLANES))
        def _():
            for half in range(2):
                arrived(first_a.at[s2, half], r1_recv.at[s2, half, 0])
                arrived(first_b.at[s2, half], r1_recv.at[s2, half, 1])
            total_a = paired[s2, x, :, : WIDTH // 2, :].astype(jnp.float32)
            total_b = paired[s2, :, y, WIDTH // 2 :, :].astype(jnp.float32)
            for half in range(2):
                total_a += wide(first_a, s2, half)
                total_b += wide(first_b, s2, half)
            joined_a[s2] = total_a.astype(jnp.bfloat16)
            joined_b[s2] = total_b.astype(jnp.bfloat16)
            for step in range(1, SIDE):
                for copy in second_exchange(s2, step):
                    copy.start()

        s3 = PLANES - 1 - (t - LAG_SECOND)

        @pl.when((s3 >= 0) & (s3 < PLANES))
        def _():
            for step in range(1, SIDE):
                arrived(second_a.at[s3, step - 1], r2_recv.at[s3, step, 0])
                arrived(second_b.at[s3, step - 1], r2_recv.at[s3, step, 1])
            total_a = wide(joined_a, s3, y)
            total_b = wide(joined_b, s3, x)
            for step in range(SIDE - 1):
                total_a += wide(second_a, s3, step)
                total_b += wide(second_b, s3, step)
            total = jnp.concatenate([total_a, total_b], axis=0).astype(jnp.bfloat16)

            @pl.when(s3 != z)
            def _():
                square[s3] = total
                to_plane(s3).start()

            @pl.when(s3 == z)
            def _():
                planes[z] = total

            pair_exchange(s3).wait_send()
            for copy in by_way(s3) + first_exchange(s3):
                copy.wait_send()

        for at, tap_step in enumerate(tap_steps):
            pl.when(t == PLANES + LAG_SECOND - len(tap_steps) + at)(tap_step)

        return carry

    lax.fori_loop(0, PLANES + LAG_SECOND, backward_step, 0)

    for copy in to_next_plane(1) + to_next_plane(-1):
        copy.wait_send()
    for hops in (1, 2, 3):
        for i in range(PIECES):
            for copy in relays(hops, i):
                copy.wait_send()

    def left_sums(s, carry):
        for step in range(1, SIDE):
            for copy in second_exchange(s, step):
                copy.wait_send()
        return carry

    lax.fori_loop(0, PLANES, left_sums, 0)
    tap_swap(tap_twin, 0).wait_send()
    for step in range(1, SIDE):
        tap_side(tap_x, x, step, 1, dx=step).wait_send()
        tap_side(tap_y, y, step, 2, dy=step).wait_send()

    def left_planes(s):
        arrived(planes.at[s], r3_recv.at[s])
        taps_to_plane(s).wait_send()
        to_plane(s).wait_send()

    others(left_planes)
    total = wide(planes, 0)
    for s in range(1, PLANES):
        total += wide(planes, s)
    out_point[...] = total.reshape(SECTION, SECTION, CHANNELS)
    arrived(tap_final.at[1 - core], te_recv.at[3, 0])
    for side in range(2):
        out_taps[:, :, side * HALF : (side + 1) * HALF] = tap_final[side]
    tap_swap(tap_final, 3).wait_send()


def per_device(images, cotangent, section_cells, point_weight, tap_weight):
    cells = PLANES * SECTION
    bf16, f32 = jnp.bfloat16, jnp.float32
    vmem, dma = pltpu.VMEM, pltpu.SemaphoreType.DMA
    hbm_spec = pl.BlockSpec(memory_space=pl.ANY)
    vmem_spec = pl.BlockSpec(memory_space=pltpu.VMEM)
    block = (WIDTH, CHANNELS)
    half_block = (WIDTH // 2, CHANNELS)
    tap_block = (3, SECTION, CHANNELS)
    tap_half = (3, SECTION, HALF)
    scratch = [
        vmem((cells, CHANNELS, CHANNELS), bf16),
        vmem((PLANES,) + tap_block, f32),
        vmem((cells,) + block, bf16),
        vmem((cells,) + block, bf16),
        vmem((cells,) + block, f32),
        vmem(block, bf16),
        vmem(block, bf16),
        vmem(block, bf16),
        vmem(block, f32),
        vmem((PLANES, SIDE, SIDE, 2) + block, bf16),
        vmem((PLANES, SIDE, SIDE) + block, bf16),
        vmem((PLANES, SIDE, SIDE) + block, bf16),
        vmem((PLANES, 2, 2) + half_block, bf16),
        vmem((PLANES, 2, 2) + half_block, bf16),
        vmem((PLANES, 2, SIDE) + half_block, bf16),
        vmem((PLANES, 2, SIDE) + half_block, bf16),
        vmem((PLANES, SIDE) + half_block, bf16),
        vmem((PLANES, SIDE) + half_block, bf16),
        vmem((PLANES, SIDE - 1) + half_block, bf16),
        vmem((PLANES, SIDE - 1) + half_block, bf16),
        vmem((PLANES,) + block, bf16),
        vmem((PLANES,) + block, bf16),
        vmem((PLANES,) + tap_block, f32),
        vmem((PLANES,) + tap_block, f32),
        vmem((2,) + tap_block, f32),
        vmem((SIDE,) + tap_half, f32),
        vmem((SIDE,) + tap_half, f32),
        vmem((2,) + tap_half, f32),
        dma((3,)),
    ]
    for shape in (
        (PLANES + 1, PIECES), (PLANES, 2, 2), (PLANES, 2, 2), (PLANES, 2),
        (PLANES,), (PLANES, 2, 2), (PLANES, 2, 2), (PLANES, SIDE, 2), (PLANES,),
        (PLANES,), (SIDE, SIDE),
    ):
        scratch += [dma(shape), dma(shape)]
    grad_point, grad_taps = pl.pallas_call(
        window_kernel,
        out_shape=(
            jax.ShapeDtypeStruct((SECTION, SECTION, CHANNELS), f32),
            jax.ShapeDtypeStruct(tap_block, f32),
        ),
        in_specs=[pl.BlockSpec(memory_space=pltpu.SMEM), hbm_spec, hbm_spec, hbm_spec, vmem_spec],
        out_specs=(vmem_spec, vmem_spec),
        scratch_shapes=scratch,
        compiler_params=pltpu.CompilerParams(
            collective_id=0, has_side_effects=True, vmem_limit_bytes=56 << 20
        ),
    )(section_cells, images, cotangent, point_weight, jnp.swapaxes(tap_weight, 0, 1))
    return grad_point, jnp.swapaxes(grad_taps, 0, 1)


def solution(mesh):
    placed = (
        P(None, "dp", None, None),
        P(None, "dp", None, None),
        P(),
        P("segment", None, None),
        P("segment", None, None),
    )
    return jax.shard_map(
        per_device,
        mesh=mesh,
        in_specs=placed,
        out_specs=(P("segment", "dp", None), P("segment", None, None)),
        check_vma=False,
    )
```

```python
import jax
import jax.numpy as jnp
from jax import lax
from jax.experimental import pallas as pl
from jax.experimental.pallas import tpu as pltpu
from jax.sharding import PartitionSpec as P

SECTION = 8
PLANES = 8
SIDE = 4
WIDTH = 64
CHANNELS = 256
HALF = CHANNELS // 2
QUARTER = CHANNELS // 4
EIGHTH = CHANNELS // 8
PIECES = 5
MOST_RUNS = 2
RING_STEPS = (0, 2, 3, 4)
LAG_SUM = 1
LAG_NEAR = 3
LAG_FIRST = 5
LAG_SECOND = 7
LAG_ACROSS = 2
LAG_TWIN = 4
VISITS = PLANES - 1 + LAG_TWIN


def arrival_orders():
    orders, runs = [], []
    for plane in range(PLANES):
        left = [s for s in range(PLANES) if s != plane]
        hops = {s: min((s - plane) % PLANES, (plane - s) % PLANES) for s in left}
        order = []
        while left:
            reach = sum(step <= len(order) for step in RING_STEPS)
            order.append(min(s for s in left if hops[s] <= reach))
            left.remove(order[-1])
        done, counts = 0, []
        for step in range(VISITS):
            count = 0
            while done < PLANES and (done == plane or order.index(done) < step - LAG_TWIN):
                if count == MOST_RUNS:
                    break
                count, done = count + 1, done + 1
            counts.append(count)
        orders.append(sum(s * 8**i for i, s in enumerate(order)))
        runs.append(sum(n * 4**i for i, n in enumerate(counts)))
    return orders, runs


def by_plane(z, values):
    chosen = values[0]
    for plane in range(1, PLANES):
        chosen = jnp.where(z == plane, values[plane], chosen)
    return chosen


def neighbours(values, dilation):
    count = values.shape[0]
    place = lax.broadcasted_iota(jnp.int32, values.shape, 0)
    before = jnp.where(place >= dilation, pltpu.roll(values, dilation, 0), 0.0)
    beyond = jnp.where(place < count - dilation, pltpu.roll(values, count - dilation, 0), 0.0)
    return before, beyond


def window_kernel(
    section_cells, images, cotangent, point_weight, tap_weight,
    out_point, out_taps,
    weight, taps, inputs, active, slope, image, grad_row, x_now, g_now,
    partial, from_twin, paired, far_a, far_b, first_a, first_b, joined_a, joined_b,
    second_a, second_b, square, planes,
    tap_grads, tap_planes, tap_twin, tap_x, tap_y, tap_final,
    local_sem,
    gz_send, gz_recv, g1_send, g1_recv, g2_send, g2_recv, gt_send, gt_recv,
    rt_send, rt_recv, rf_send, rf_recv, r1_send, r1_recv, r2_send, r2_recv, r3_send, r3_recv,
    tz_send, tz_recv, te_send, te_recv,
):
    z = lax.axis_index("segment")
    dp = lax.axis_index("dp")
    x, y, core = dp // 8, (dp // 2) % SIDE, dp % 2

    def device(dz=0, dx=0, dy=0, dc=0):
        px, py = (x + dx + SIDE) % SIDE, (y + dy + SIDE) % SIDE
        return ((z + dz + PLANES) % PLANES, (px * SIDE + py) * 2 + (core + dc) % 2)

    twin = device(dc=1)

    def remote(src, dst, send, recv, target):
        return pltpu.make_async_remote_copy(
            src_ref=src, dst_ref=dst, send_sem=send, recv_sem=recv,
            device_id=target, device_id_type=pl.DeviceIdType.MESH,
        )

    own_row = pltpu.make_async_copy(images.at[z // 2, z % 2], image, local_sem.at[0])
    own_grad = pltpu.make_async_copy(cotangent.at[z // 2, z % 2], grad_row, local_sem.at[1])
    own_weight = pltpu.make_async_copy(
        point_weight, weight.at[pl.ds(z * SECTION, SECTION)], local_sem.at[2]
    )
    own_row.start()
    own_grad.start()
    own_weight.start()
    taps[z] = tap_weight[...]

    barrier = pltpu.get_barrier_semaphore()
    partners = [twin]
    partners += [device(dz=step) for step in range(1, PLANES)]
    partners += [device(dx=step) for step in range(1, SIDE)]
    partners += [device(dy=step) for step in range(1, SIDE)]
    for partner in partners:
        pl.semaphore_signal(
            barrier, inc=1, device_id=partner, device_id_type=pl.DeviceIdType.MESH
        )
    pl.semaphore_wait(barrier, len(partners))

    base = core * HALF
    rows_a = pl.ds(pl.multiple_of(base + (y % 2) * QUARTER, QUARTER), QUARTER)
    rows_b = pl.ds(pl.multiple_of(base + (x % 2) * QUARTER, QUARTER), QUARTER)
    other_a = pl.ds(pl.multiple_of(base + (1 - y % 2) * QUARTER, QUARTER), QUARTER)
    other_b = pl.ds(pl.multiple_of(base + (1 - x % 2) * QUARTER, QUARTER), QUARTER)
    start_a, start_b = base + (y % 2) * QUARTER, base + (x % 2) * QUARTER
    part_a = pl.ds(pl.multiple_of(start_a + (x % 2) * EIGHTH, EIGHTH), EIGHTH)
    part_b = pl.ds(pl.multiple_of(start_b + (y % 2) * EIGHTH, EIGHTH), EIGHTH)
    missing_a = pl.ds(pl.multiple_of(start_a + (1 - x % 2) * EIGHTH, EIGHTH), EIGHTH)
    missing_b = pl.ds(pl.multiple_of(start_b + (1 - y % 2) * EIGHTH, EIGHTH), EIGHTH)
    rows_core = pl.ds(pl.multiple_of(base, HALF), HALF)
    rows_twin = pl.ds(pl.multiple_of(HALF - base, HALF), HALF)
    lanes_core, lanes_twin = rows_core, rows_twin

    def pieces(s):
        return (
            weight.at[pl.ds(s * SECTION, 2), part_a],
            weight.at[pl.ds(s * SECTION + 2, 2), part_a],
            weight.at[pl.ds(s * SECTION + 4, 2), part_b],
            weight.at[pl.ds(s * SECTION + 6, 2), part_b],
            taps.at[s, :, :, lanes_core],
        )

    def to_next_plane(direction):
        sources = (
            point_weight.at[pl.ds(0, 2), part_a], point_weight.at[pl.ds(2, 2), part_a],
            point_weight.at[pl.ds(4, 2), part_b], point_weight.at[pl.ds(6, 2), part_b],
            tap_weight.at[:, :, lanes_core],
        )
        at = z if direction == 1 else PLANES
        return [
            remote(source, piece, gz_send.at[at, i], gz_recv.at[z, i], device(dz=direction))
            for i, (source, piece) in enumerate(zip(sources, pieces(z)))
        ]

    def relays(hops, i):
        last = ((0, 1, 4), (2, 3))
        directions = [d for at, d in enumerate((1, -1)) if hops < 3 or i in last[at]]
        copies = []
        for direction in directions:
            s = (z - direction * hops + PLANES) % PLANES
            piece = pieces(s)[i]
            copies.append(
                remote(piece, piece, gz_send.at[s, i], gz_recv.at[s, i], device(dz=direction))
            )
        return copies

    def arrived(ref, sem):
        pltpu.make_async_copy(ref, ref, sem).wait()

    def along_side(s):
        copies = []
        for low, direction in ((0, 1), (2, -1)):
            piece_a = weight.at[pl.ds(s * SECTION + low, 2), part_a]
            piece_b = weight.at[pl.ds(s * SECTION + SIDE + low, 2), part_b]
            at = low // 2
            copies.append(
                remote(piece_a, piece_a, g1_send.at[s, at, 0], g1_recv.at[s, at, 0], device(dx=direction))
            )
            copies.append(
                remote(piece_b, piece_b, g1_send.at[s, at, 1], g1_recv.at[s, at, 1], device(dy=direction))
            )
        return copies

    def across_side(s):
        copies = []
        for low, direction in ((0, 1), (2, -1)):
            piece_a = weight.at[pl.ds(s * SECTION + low, 2), rows_a]
            piece_b = weight.at[pl.ds(s * SECTION + SIDE + low, 2), rows_b]
            at = low // 2
            copies.append(
                remote(piece_a, piece_a, g2_send.at[s, at, 0], g2_recv.at[s, at, 0], device(dy=direction))
            )
            copies.append(
                remote(piece_b, piece_b, g2_send.at[s, at, 1], g2_recv.at[s, at, 1], device(dx=direction))
            )
        return copies

    def to_twin(s):
        half = weight.at[pl.ds(s * SECTION, SECTION), rows_core]
        lanes = taps.at[s, :, :, lanes_core]
        return (
            remote(half, half, gt_send.at[s, 0], gt_recv.at[s, 0], twin),
            remote(lanes, lanes, gt_send.at[s, 1], gt_recv.at[s, 1], twin),
        )

    for copies in zip(to_next_plane(1), to_next_plane(-1)):
        for copy in copies:
            copy.start()

    def forward(s, slot, member, dilation, field):
        values = field.astype(jnp.float32)
        live = jnp.full(values.shape, section_cells[s]) > member
        before, beyond = neighbours(values, dilation)
        rows = [taps[s, tap, member : member + 1, :] for tap in range(3)]
        hidden = rows[0] * before + rows[1] * values + rows[2] * beyond
        sigmoid = 0.5 * jnp.tanh(0.5 * hidden) + 0.5
        product = hidden * sigmoid
        activated = jnp.where(live, product, 0.0).astype(jnp.bfloat16)
        inputs[slot] = field
        active[slot] = activated
        slope[slot] = jnp.where(live, sigmoid + product * (1.0 - sigmoid), 0.0)
        branch = jnp.dot(activated, weight[slot], preferred_element_type=jnp.float32)
        return (values + branch).astype(jnp.bfloat16)

    own_row.wait()
    x_now[...] = image[...]

    orders, runs = arrival_orders()

    def run_section(s, carry):
        @pl.when(s != z)
        def _():
            arrived(weight.at[pl.ds(s * SECTION, SECTION), rows_twin], gt_recv.at[s, 0])
            arrived(taps.at[s, :, :, lanes_twin], gt_recv.at[s, 1])

        @pl.when(s == z)
        def _():
            own_weight.wait()

        field = x_now[...]
        for member in range(SECTION):
            field = forward(s, s * SECTION + member, member, 1 + member % 2, field)
        x_now[...] = field
        return carry

    def gather_step(t, carry):
        order, run, done, *seen = carry
        s0 = order % 8
        seen = [s0] + seen
        s1, s2 = seen[LAG_ACROSS], seen[LAG_TWIN]

        for hops, at in enumerate(RING_STEPS, 1):

            @pl.when(t == at)
            def _():
                for i in range(PIECES):
                    for s in {4: (z + hops,)}.get(hops, (z - hops + PLANES, z + hops)):
                        arrived(pieces(s % PLANES)[i], gz_recv.at[s % PLANES, i])
                    if hops < 4:
                        for copy in relays(hops, i):
                            copy.start()

        @pl.when(t < PLANES - 1)
        def _():
            for copy in along_side(s0):
                copy.start()

        @pl.when((t >= LAG_ACROSS) & (t < LAG_ACROSS + PLANES - 1))
        def _():
            for low in (0, 2):
                arrived(weight.at[pl.ds(s1 * SECTION + low, 2), missing_a], g1_recv.at[s1, low // 2, 0])
                arrived(
                    weight.at[pl.ds(s1 * SECTION + SIDE + low, 2), missing_b],
                    g1_recv.at[s1, low // 2, 1],
                )
            for copy in across_side(s1):
                copy.start()

        @pl.when(t >= LAG_TWIN)
        def _():
            for low in (0, 2):
                arrived(weight.at[pl.ds(s2 * SECTION + low, 2), other_a], g2_recv.at[s2, low // 2, 0])
                arrived(
                    weight.at[pl.ds(s2 * SECTION + SIDE + low, 2), other_b],
                    g2_recv.at[s2, low // 2, 1],
                )
            for copy in to_twin(s2):
                copy.start()

        after = done + run % 4
        lax.fori_loop(done, after, run_section, 0)
        return (order // 8, run // 4, after, *seen[:-1])

    start = (by_plane(z, orders), by_plane(z, runs)) + (z * 0,) * (LAG_TWIN + 1)
    done = lax.fori_loop(0, VISITS, gather_step, start)[2]
    lax.fori_loop(done, PLANES, run_section, 0)

    def pair_exchange(s, upper):
        cells = pl.ds(upper * (WIDTH // 2), WIDTH // 2)
        return remote(
            partial.at[s, :, :, 1 - core, cells], from_twin.at[s, :, :, cells],
            rt_send.at[s, upper], rt_recv.at[s, upper], twin,
        )

    low, high = pl.ds(0, WIDTH // 2), pl.ds(WIDTH // 2, WIDTH // 2)

    def by_way(s):
        copies = []
        for half, direction in enumerate((1, -1)):
            two = pl.ds(2 * half, 2)
            copies += [
                remote(
                    paired.at[s, (x + 2) % SIDE, two, low], far_a.at[s, half],
                    rf_send.at[s, half, 0], rf_recv.at[s, half, 0], device(dx=direction),
                ),
                remote(
                    paired.at[s, two, (y + 2) % SIDE, high], far_b.at[s, half],
                    rf_send.at[s, half, 1], rf_recv.at[s, half, 1], device(dy=direction),
                ),
            ]
        return copies

    def first_exchange(s):
        copies = []
        for half, direction in enumerate((1, -1)):
            copies += [
                remote(
                    paired.at[s, (x + direction + SIDE) % SIDE, :, low], first_a.at[s, half],
                    r1_send.at[s, half, 0], r1_recv.at[s, half, 0], device(dx=direction),
                ),
                remote(
                    paired.at[s, :, (y + direction + SIDE) % SIDE, high], first_b.at[s, half],
                    r1_send.at[s, half, 1], r1_recv.at[s, half, 1], device(dy=direction),
                ),
            ]
        return copies

    def second_exchange(s, step):
        return (
            remote(
                joined_a.at[s, (y + step) % SIDE], second_a.at[s, step - 1],
                r2_send.at[s, step, 0], r2_recv.at[s, step, 0], device(dy=step),
            ),
            remote(
                joined_b.at[s, (x + step) % SIDE], second_b.at[s, step - 1],
                r2_send.at[s, step, 1], r2_recv.at[s, step, 1], device(dx=step),
            ),
        )

    def to_plane(s):
        return remote(
            square.at[s], planes.at[z], r3_send.at[s], r3_recv.at[z], (s, dp)
        )

    def taps_to_plane(s):
        return remote(
            tap_grads.at[s], tap_planes.at[z], tz_send.at[s], tz_recv.at[z], (s, dp)
        )

    def backward(s, slot, member, dilation, upstream):
        rounded = upstream.astype(jnp.bfloat16)
        grad_active = lax.dot_general(
            rounded, weight[slot], (((1,), (1,)), ((), ())), preferred_element_type=jnp.float32
        )
        live = jnp.full(grad_active.shape, section_cells[s]) > member
        grad_hidden = jnp.where(live, grad_active * slope[slot], 0.0)
        spread_before, spread_beyond = neighbours(grad_hidden, dilation)
        values = inputs[slot].astype(jnp.float32)
        for tap, spread in enumerate((spread_beyond, grad_hidden, spread_before)):
            tap_grads[s, tap, member : member + 1, :] = jnp.sum(spread * values, axis=0, keepdims=True)
        grad_matrix = lax.dot_general(
            active[slot], rounded, (((0,), (0,)), ((), ())), preferred_element_type=jnp.float32
        )
        rows = [taps[s, tap, member : member + 1, :] for tap in range(3)]
        passed = (
            upstream + rows[0] * spread_beyond + rows[1] * grad_hidden + rows[2] * spread_before
        )
        return passed, grad_matrix.reshape(PLANES * SIDE, SECTION, CHANNELS)

    own_grad.wait()
    g_now[...] = grad_row[...].astype(jnp.float32)

    def others(body):
        def visit(s, carry):
            @pl.when(s != z)
            def _():
                body(s)

            return carry

        lax.fori_loop(0, PLANES, visit, 0)

    def tap_side(buffer, place, step, at, **offset):
        return remote(
            buffer.at[place], buffer.at[place], te_send.at[at, step], te_recv.at[at, step],
            device(**offset),
        )

    def tap_swap(buffer, at):
        return remote(buffer.at[core], buffer.at[core], te_send.at[at, 0], te_recv.at[at, 0], twin)

    def tap_cores():
        others(lambda s: arrived(tap_planes.at[s], tz_recv.at[s]))
        total = tap_planes[0]
        for s in range(1, PLANES):
            total += tap_planes[s]
        tap_twin[core] = total
        tap_swap(tap_twin, 0).start()

    def tap_along_x():
        arrived(tap_twin.at[1 - core], te_recv.at[0, 0])
        tap_x[x] = tap_twin[0, :, :, lanes_core] + tap_twin[1, :, :, lanes_core]
        for step in range(1, SIDE):
            tap_side(tap_x, x, step, 1, dx=step).start()

    def tap_along_y():
        for step in range(1, SIDE):
            arrived(tap_x.at[(x + SIDE - step) % SIDE], te_recv.at[1, step])
        tap_y[y] = (tap_x[0] + tap_x[1]) + (tap_x[2] + tap_x[3])
        for step in range(1, SIDE):
            tap_side(tap_y, y, step, 2, dy=step).start()

    def tap_halves():
        for step in range(1, SIDE):
            arrived(tap_y.at[(y + SIDE - step) % SIDE], te_recv.at[2, step])
        tap_final[core] = (tap_y[0] + tap_y[1]) + (tap_y[2] + tap_y[3])
        tap_swap(tap_final, 3).start()

    tap_steps = (tap_cores, tap_along_x, tap_along_y, tap_halves)

    def wide(ref, *index):
        return ref[index].astype(jnp.float32)

    def backward_step(t, carry):
        @pl.when(t < PLANES)
        def _():
            s = PLANES - 1 - t

            upstream = g_now[...]
            for p in reversed(range(SECTION // 2)):
                slot = s * SECTION + 2 * p
                upstream, odd = backward(s, slot + 1, 2 * p + 1, 2, upstream)
                upstream, even = backward(s, slot, 2 * p, 1, upstream)
                both = jnp.concatenate([even, odd], axis=1).astype(jnp.bfloat16)
                partial[s, :, :, :, 16 * p : 16 * p + 16, :] = both.reshape(
                    SIDE, SIDE, 2, 16, CHANNELS
                )
                if p == 2:
                    pair_exchange(s, 1).start()
            g_now[...] = upstream
            pair_exchange(s, 0).start()

            @pl.when(s != z)
            def _():
                taps_to_plane(s).start()

            @pl.when(s == z)
            def _():
                tap_planes[z] = tap_grads[z]

            @pl.when(t != z)
            def _():
                for copy in along_side(t) + across_side(t) + list(to_twin(t)):
                    copy.wait_send()

        s1 = PLANES - 1 - (t - LAG_SUM)

        @pl.when((s1 >= 0) & (s1 < PLANES))
        def _():
            arrived(from_twin.at[s1, :, :, low], rt_recv.at[s1, 0])
            arrived(from_twin.at[s1, :, :, high], rt_recv.at[s1, 1])

            def add(i, carry):
                paired[s1, i] = (wide(partial, s1, i, slice(None), core) + wide(from_twin, s1, i)).astype(
                    jnp.bfloat16
                )
                return carry

            lax.fori_loop(0, SIDE, add, 0)
            for copy in by_way(s1):
                copy.start()

        near = PLANES - 1 - (t - LAG_NEAR)

        @pl.when((near >= 0) & (near < PLANES))
        def _():
            for half, direction in enumerate((1, -1)):
                px, py = (x + direction + SIDE) % SIDE, (y + direction + SIDE) % SIDE
                arrived(far_a.at[near, half], rf_recv.at[near, half, 0])
                arrived(far_b.at[near, half], rf_recv.at[near, half, 1])
                for i in range(2):
                    at = 2 * half + i
                    own_a = paired[near, px, at, : WIDTH // 2, :].astype(jnp.float32)
                    own_b = paired[near, at, py, WIDTH // 2 :, :].astype(jnp.float32)
                    paired[near, px, at, : WIDTH // 2, :] = (
                        own_a + wide(far_a, near, half, i)
                    ).astype(jnp.bfloat16)
                    paired[near, at, py, WIDTH // 2 :, :] = (
                        own_b + wide(far_b, near, half, i)
                    ).astype(jnp.bfloat16)
            for copy in first_exchange(near):
                copy.start()

        s2 = PLANES - 1 - (t - LAG_FIRST)

        @pl.when((s2 >= 0) & (s2 < PLANES))
        def _():
            for half in range(2):
                arrived(first_a.at[s2, half], r1_recv.at[s2, half, 0])
                arrived(first_b.at[s2, half], r1_recv.at[s2, half, 1])
            total_a = paired[s2, x, :, : WIDTH // 2, :].astype(jnp.float32)
            total_b = paired[s2, :, y, WIDTH // 2 :, :].astype(jnp.float32)
            for half in range(2):
                total_a += wide(first_a, s2, half)
                total_b += wide(first_b, s2, half)
            joined_a[s2] = total_a.astype(jnp.bfloat16)
            joined_b[s2] = total_b.astype(jnp.bfloat16)
            for step in range(1, SIDE):
                for copy in second_exchange(s2, step):
                    copy.start()

        s3 = PLANES - 1 - (t - LAG_SECOND)

        @pl.when((s3 >= 0) & (s3 < PLANES))
        def _():
            for step in range(1, SIDE):
                arrived(second_a.at[s3, step - 1], r2_recv.at[s3, step, 0])
                arrived(second_b.at[s3, step - 1], r2_recv.at[s3, step, 1])
            total_a = wide(joined_a, s3, y)
            total_b = wide(joined_b, s3, x)
            for step in range(SIDE - 1):
                total_a += wide(second_a, s3, step)
                total_b += wide(second_b, s3, step)
            total = jnp.concatenate([total_a, total_b], axis=0).astype(jnp.bfloat16)

            @pl.when(s3 != z)
            def _():
                square[s3] = total
                to_plane(s3).start()

            @pl.when(s3 == z)
            def _():
                planes[z] = total

            pair_exchange(s3, 0).wait_send()
            pair_exchange(s3, 1).wait_send()
            for copy in by_way(s3) + first_exchange(s3):
                copy.wait_send()

        for at, tap_step in enumerate(tap_steps):
            pl.when(t == PLANES + LAG_SECOND - len(tap_steps) + at)(tap_step)

        return carry

    lax.fori_loop(0, PLANES + LAG_SECOND, backward_step, 0)

    for copy in to_next_plane(1) + to_next_plane(-1):
        copy.wait_send()
    for hops in (1, 2, 3):
        for i in range(PIECES):
            for copy in relays(hops, i):
                copy.wait_send()

    def left_sums(s, carry):
        for step in range(1, SIDE):
            for copy in second_exchange(s, step):
                copy.wait_send()
        return carry

    lax.fori_loop(0, PLANES, left_sums, 0)
    tap_swap(tap_twin, 0).wait_send()
    for step in range(1, SIDE):
        tap_side(tap_x, x, step, 1, dx=step).wait_send()
        tap_side(tap_y, y, step, 2, dy=step).wait_send()

    def left_planes(s):
        arrived(planes.at[s], r3_recv.at[s])
        taps_to_plane(s).wait_send()
        to_plane(s).wait_send()

    others(left_planes)
    total = wide(planes, 0)
    for s in range(1, PLANES):
        total += wide(planes, s)
    out_point[...] = total.reshape(SECTION, SECTION, CHANNELS)
    arrived(tap_final.at[1 - core], te_recv.at[3, 0])
    for side in range(2):
        out_taps[:, :, side * HALF : (side + 1) * HALF] = tap_final[side]
    tap_swap(tap_final, 3).wait_send()


def per_device(images, cotangent, section_cells, point_weight, tap_weight):
    cells = PLANES * SECTION
    bf16, f32 = jnp.bfloat16, jnp.float32
    vmem, dma = pltpu.VMEM, pltpu.SemaphoreType.DMA
    hbm_spec = pl.BlockSpec(memory_space=pl.ANY)
    vmem_spec = pl.BlockSpec(memory_space=pltpu.VMEM)
    block = (WIDTH, CHANNELS)
    half_block = (WIDTH // 2, CHANNELS)
    tap_block = (3, SECTION, CHANNELS)
    tap_half = (3, SECTION, HALF)
    scratch = [
        vmem((cells, CHANNELS, CHANNELS), bf16),
        vmem((PLANES,) + tap_block, f32),
        vmem((cells,) + block, bf16),
        vmem((cells,) + block, bf16),
        vmem((cells,) + block, f32),
        vmem(block, bf16),
        vmem(block, bf16),
        vmem(block, bf16),
        vmem(block, f32),
        vmem((PLANES, SIDE, SIDE, 2) + block, bf16),
        vmem((PLANES, SIDE, SIDE) + block, bf16),
        vmem((PLANES, SIDE, SIDE) + block, bf16),
        vmem((PLANES, 2, 2) + half_block, bf16),
        vmem((PLANES, 2, 2) + half_block, bf16),
        vmem((PLANES, 2, SIDE) + half_block, bf16),
        vmem((PLANES, 2, SIDE) + half_block, bf16),
        vmem((PLANES, SIDE) + half_block, bf16),
        vmem((PLANES, SIDE) + half_block, bf16),
        vmem((PLANES, SIDE - 1) + half_block, bf16),
        vmem((PLANES, SIDE - 1) + half_block, bf16),
        vmem((PLANES,) + block, bf16),
        vmem((PLANES,) + block, bf16),
        vmem((PLANES,) + tap_block, f32),
        vmem((PLANES,) + tap_block, f32),
        vmem((2,) + tap_block, f32),
        vmem((SIDE,) + tap_half, f32),
        vmem((SIDE,) + tap_half, f32),
        vmem((2,) + tap_half, f32),
        dma((3,)),
    ]
    for shape in (
        (PLANES + 1, PIECES), (PLANES, 2, 2), (PLANES, 2, 2), (PLANES, 2),
        (PLANES, 2), (PLANES, 2, 2), (PLANES, 2, 2), (PLANES, SIDE, 2), (PLANES,),
        (PLANES,), (SIDE, SIDE),
    ):
        scratch += [dma(shape), dma(shape)]
    grad_point, grad_taps = pl.pallas_call(
        window_kernel,
        out_shape=(
            jax.ShapeDtypeStruct((SECTION, SECTION, CHANNELS), f32),
            jax.ShapeDtypeStruct(tap_block, f32),
        ),
        in_specs=[pl.BlockSpec(memory_space=pltpu.SMEM), hbm_spec, hbm_spec, hbm_spec, vmem_spec],
        out_specs=(vmem_spec, vmem_spec),
        scratch_shapes=scratch,
        compiler_params=pltpu.CompilerParams(
            collective_id=0, has_side_effects=True, vmem_limit_bytes=56 << 20
        ),
    )(section_cells, images, cotangent, point_weight, jnp.swapaxes(tap_weight, 0, 1))
    return grad_point, jnp.swapaxes(grad_taps, 0, 1)


def solution(mesh):
    placed = (
        P(None, "dp", None, None),
        P(None, "dp", None, None),
        P(),
        P("segment", None, None),
        P("segment", None, None),
    )
    return jax.shard_map(
        per_device,
        mesh=mesh,
        in_specs=placed,
        out_specs=(P("segment", "dp", None), P("segment", None, None)),
        check_vma=False,
    )
```
